256 devices in a mesh: batch: 128 (over z, y, x_lo, core), rows: 2 (over x_hi).
Axes of the slice: x: 4 (x_hi: 2, x_lo: 2; x = x_hi * 2 + x_lo), y: 4, z: 8, core: 2. Of those that a mesh axis runs over, the one named last changes fastest.
Arguments:
- block_input: bfloat16 [128, 16, 64, 384], P('batch', 'rows'), may hold values from -6 to 6
- output_grad: bfloat16 [128, 16, 64, 768], P('batch', 'rows'), may hold values from -6 to 6
- conv_weight: float32 [384, 1152], P(None, 'batch'), may hold values from -12 to 12
- conv_gain: float32 [384], replicated, may hold values from 0.1 to 1.9
- conv_momentum: float32 [384, 1152], P(None, 'batch'), may hold values from -0.6 to 0.6
- proj_weight: float32 [768, 384], P(None, 'batch'), may hold values from -12 to 12
- proj_gain: float32 [768], replicated, may hold values from 0.1 to 1.9
- proj_momentum: float32 [768, 384], P(None, 'batch'), may hold values from -0.6 to 0.6
Outputs:
- input_grad: bfloat16 [128, 16, 64, 384], P('batch', 'rows')
- new_conv_weight: float32 [384, 1152], P(None, 'batch')
- new_conv_momentum: float32 [384, 1152], P(None, 'batch')
- new_proj_weight: float32 [768, 384], P(None, 'batch')
- new_proj_momentum: float32 [768, 384], P(None, 'batch')
The draws below stay inside these ranges and needn't reach their ends.
All inputs are finite; a program needn't handle non-finite values.
Results may differ from the reference program's by a relative error of at most 0.0031.
The reference program's roundings to bfloat16 on the way (of `standard`, `activated`, `hidden` and `pre_grad`) count: a program that leaves them out, or rounds other values in their place, can miss the bound.
Values may be sent and summed in bfloat16 or wider, within the bound.
No kernel may reach another device: no remote copies, remote signals or barrier semaphores. Data moves between devices by JAX's collectives and lax.ppermute only.
A program may use at most 64 MiB of HBM per device.

```python
import math
import jax
import jax.numpy as jnp
from jax import lax

CH = 384
GW = 128
OUT = 768
COLS = 64
IMAGES = 128
MAP_ROWS = 16


def scaled_rows(key, row_count, col_count):
    key_scale, key_body = jax.random.split(key)
    log_scale = jax.random.uniform(key_scale, (row_count, 1), jnp.float32, math.log(0.3), math.log(3.0))
    values = jax.random.truncated_normal(key_body, -4.0, 4.0, (row_count, col_count), jnp.float32)
    return jnp.exp(log_scale) * values


def draw_conv_weight(key, part):
    return scaled_rows(jax.random.fold_in(key, 11), CH, 9 * GW)


def draw_proj_weight(key, part):
    return scaled_rows(jax.random.fold_in(key, 23), OUT, CH)


def levels(stream_key, shape, pieces, low, largest):
    def one(axis_at, parts):
        heights = jax.random.uniform(jax.random.fold_in(jax.random.fold_in(stream_key, 6), axis_at), (parts,), jnp.float32, low / len(pieces), largest / len(pieces))
        return jnp.repeat(jnp.exp(heights), shape[axis_at] // parts).reshape((-1,) + (1,) * (len(shape) - axis_at - 1))

    level = one(*pieces[0])
    for cut in pieces[1:]:
        level = level * one(*cut)
    return level


def normal_values(stream_key, dims, width, most, cuts=(), dtype=jnp.bfloat16):
    factor_of = levels(stream_key, dims, cuts, -0.22, 0.18) if cuts else 1.0
    values = jax.random.normal(stream_key, dims, jnp.float32) * width * factor_of
    return jnp.minimum(jnp.maximum(values, -most), most).astype(dtype)


def setup_inputs(seed: int = 0) -> dict:
    arg_keys = jax.random.split(jax.random.key(seed), 9)
    return {
        "block_input": normal_values(arg_keys[0], (IMAGES, MAP_ROWS, COLS, CH), 1.0, 6.0, ((0, 128), (1, 2))),
        "output_grad": normal_values(arg_keys[1], (IMAGES, MAP_ROWS, COLS, OUT), 1.0, 6.0, ((0, 128), (1, 2))),
        "conv_weight": draw_conv_weight(jax.random.fold_in(arg_keys[8], 71), 0),
        "conv_gain": jnp.clip(1.0 + 0.18 * jax.random.normal(arg_keys[3], (CH,), jnp.float32), 0.1, 1.9),
        "conv_momentum": normal_values(arg_keys[4], (CH, 9 * GW), 0.1, 0.6, ((1, 128),), jnp.float32),
        "proj_weight": draw_proj_weight(jax.random.fold_in(arg_keys[8], 71), 0),
        "proj_gain": jnp.clip(1.0 + 0.18 * jax.random.normal(arg_keys[6], (OUT,), jnp.float32), 0.1, 1.9),
        "proj_momentum": normal_values(arg_keys[7], (OUT, CH), 0.1, 0.6, ((1, 128),), jnp.float32),
    }


ws_eps = 0.0001
clip_ratio = 0.05
momentum_rate = 0.9
learn_rate = 1.6
norm_eps = 1e-06

def gelu_slope(values):
    return jax.jvp(jax.nn.gelu, (values,), (jnp.ones_like(values),))[1]

def standardize(weight, gain_row):
    center = lax.optimization_barrier(jnp.mean(weight, axis=1, keepdims=True))
    centered = weight - center
    spread = lax.optimization_barrier(jnp.sum(centered * centered, axis=1))
    factor = lax.rsqrt(spread + ws_eps)
    standard = ((gain_row * factor)[:, None] * centered).astype(jnp.bfloat16)
    return (standard, centered, factor)

def apply_update(weight, momentum, raw_grad, weight_sq, grad_sq):
    clip_scale = jnp.minimum(1.0, clip_ratio * jnp.sqrt(weight_sq) * lax.rsqrt(grad_sq + norm_eps))
    clipped = raw_grad * clip_scale[:, None]
    new_momentum = momentum_rate * momentum + clipped
    return (weight - learn_rate * (clipped + momentum_rate * new_momentum), new_momentum)

def update(weight, gain_row, momentum, centered, factor, grad_std):
    fan_in = weight.shape[1]
    grad_sum = lax.optimization_barrier(jnp.sum(grad_std, axis=1))
    grad_proj = lax.optimization_barrier(jnp.sum(grad_std * centered, axis=1))
    coef_one = gain_row * factor
    coef_two = gain_row * factor ** 3 * grad_proj
    raw_grad = coef_one[:, None] * (grad_std - (grad_sum / fan_in)[:, None]) - coef_two[:, None] * centered
    weight_sq = lax.optimization_barrier(jnp.sum(weight * weight, axis=1))
    grad_sq = lax.optimization_barrier(jnp.sum(raw_grad * raw_grad, axis=1))
    return apply_update(weight, momentum, raw_grad, weight_sq, grad_sq)

def reference(block_input, output_grad, conv_weight, conv_gain, conv_momentum, proj_weight, proj_gain, proj_momentum):
    conv_std, conv_cent, conv_factor = standardize(conv_weight, conv_gain)
    proj_std, proj_cent, proj_factor = standardize(proj_weight, proj_gain)
    groups = CH // GW
    kernel = conv_std.reshape(groups, GW, 9, GW).astype(jnp.float32)
    image_count = block_input.shape[0]
    map_rows = block_input.shape[1]
    map_cols = block_input.shape[2]
    pixels = map_rows * map_cols

    def image_step(carry, inputs):
        conv_acc, proj_acc = carry
        image, cotangent = inputs
        activated = jax.nn.gelu(image.astype(jnp.float32)).astype(jnp.bfloat16)
        padded = jnp.pad(activated, ((1, 1), (1, 1), (0, 0)))
        patch_list = []
        pre_act = jnp.zeros((pixels, groups, GW), jnp.float32)
        for position in range(9):
            top = position // 3
            left = position % 3
            patch = padded[top:top + map_rows, left:left + map_cols].reshape(pixels, groups, GW).astype(jnp.float32)
            patch_list.append(patch)
            pre_act = pre_act + jnp.einsum('pgi,goi->pgo', patch, kernel[:, :, position, :])
        pre_flat = pre_act.reshape(pixels, CH)
        hidden = jax.nn.gelu(pre_flat).astype(jnp.bfloat16)
        upstream = cotangent.reshape(pixels, OUT)
        hidden_grad = jnp.dot(upstream, proj_std, preferred_element_type=jnp.float32)
        pre_grad = (hidden_grad * gelu_slope(pre_flat)).astype(jnp.bfloat16)
        proj_acc = proj_acc + jnp.einsum('po,pi->oi', upstream.astype(jnp.float32), hidden.astype(jnp.float32))
        grad_groups = pre_grad.reshape(pixels, groups, GW).astype(jnp.float32)
        conv_terms = jnp.stack([jnp.einsum('pgi,pgo->goi', patch, grad_groups) for patch in patch_list], axis=2)
        conv_acc = conv_acc + conv_terms.reshape(CH, 9 * GW)
        grad_pad = jnp.pad(pre_grad.reshape(map_rows, map_cols, CH), ((1, 1), (1, 1), (0, 0)))
        act_grad = jnp.zeros((pixels, groups, GW), jnp.float32)
        for position in range(9):
            top = 2 - position // 3
            left = 2 - position % 3
            piece = grad_pad[top:top + map_rows, left:left + map_cols].reshape(pixels, groups, GW).astype(jnp.float32)
            act_grad = act_grad + jnp.einsum('pgo,goi->pgi', piece, kernel[:, :, position, :])
        slope = gelu_slope(image.astype(jnp.float32))
        input_grad = (act_grad.reshape(map_rows, map_cols, CH) * slope).astype(jnp.bfloat16)
        return ((conv_acc, proj_acc), input_grad)
    start = (jnp.zeros((CH, 9 * GW), jnp.float32), jnp.zeros((OUT, CH), jnp.float32))
    (conv_acc, proj_acc), input_grad = lax.scan(image_step, start, (block_input, output_grad))
    conv_grad = conv_acc / image_count
    proj_grad = proj_acc / image_count
    new_conv_weight, new_conv_momentum = update(conv_weight, conv_gain, conv_momentum, conv_cent, conv_factor, conv_grad)
    new_proj_weight, new_proj_momentum = update(proj_weight, proj_gain, proj_momentum, proj_cent, proj_factor, proj_grad)
    return (input_grad, new_conv_weight, new_conv_momentum, new_proj_weight, new_proj_momentum)
```

```python
import jax
import jax.numpy as jnp
from jax import lax
from jax.experimental import pallas as pl
from jax.experimental.pallas import tpu as pltpu
from jax.sharding import Mesh
from jax.sharding import PartitionSpec as P

CH = 384
GW = 128
OUT = 768
CONV_FAN = 9 * GW
PROJ_FAN = CH
ROWS = 8
COLS = 64
BATCH = ("z", "y", "x", "core")
PLANE = ("y", "x", "rows")

ws_eps = 0.0001
clip_ratio = 0.05
momentum_rate = 0.9
learn_rate = 1.6
norm_eps = 1e-06

F32 = jnp.float32
BF16 = jnp.bfloat16
VMEM_LIMIT = 48 * 1024 * 1024


def gelu_parts(v):
    k = 0.7978845608028654
    sq = v * v
    t = jnp.tanh(k * (v + 0.044715 * (v * sq)))
    half = 0.5 * (1.0 + t)
    slope = half + 0.5 * v * (1.0 - t * t) * (k * (1.0 + 3.0 * 0.044715 * sq))
    return v * half, slope


def shifted(v, step, col):
    n = v.shape[0]
    moved = pltpu.roll(v, (-step) % n, 0)
    edge = COLS - 1 if step > 0 else 0
    return jnp.where(col == edge, 0.0, moved)


def main_kernel(
    where_ref, wa_ref, wb_ref, x_ref, og_ref, halo_ref, cg_ref, pg_ref,
    ig_ref, own_ref, send_ref, sc_ref, sp_ref,
    wv, wc, wp, wcb, wpb, xs, acat, og9, hid, pp, psh, gc, gp, go, sems,
):
    h = where_ref[0]
    core = where_ref[1]
    first = pltpu.make_async_copy(wa_ref, wv.at[core], sems.at[0])
    second = pltpu.make_async_copy(wb_ref, wv.at[1 - core], sems.at[1])
    first.start()
    second.start()

    xs[pl.ds(1 + h, ROWS)] = x_ref[...]
    og9[pl.ds(h, ROWS)] = og_ref[...]
    zero_row = jnp.zeros((COLS, CH), BF16)

    @pl.when(h == 0)
    def _():
        xs[0] = zero_row
        xs[9] = halo_ref[0]
        xs[10] = halo_ref[1]
        og9[8, :, 0:CH] = halo_ref[2]
        og9[8, :, CH:OUT] = halo_ref[3]

    @pl.when(h == 1)
    def _():
        xs[0] = halo_ref[0]
        xs[1] = halo_ref[1]
        xs[10] = zero_row
        og9[0, :, 0:CH] = halo_ref[2]
        og9[0, :, CH:OUT] = halo_ref[3]

    col11 = lax.broadcasted_iota(jnp.int32, (11 * COLS, GW), 0) % COLS
    for g in range(3):
        lanes = slice(g * GW, (g + 1) * GW)
        act = gelu_parts(xs[:, :, lanes].reshape(11 * COLS, GW).astype(F32))[0]
        for j, piece in enumerate((shifted(act, -1, col11), act, shifted(act, 1, col11))):
            acat[g, :, :, j * GW : (j + 1) * GW] = piece.astype(BF16).reshape(11, COLS, GW)

    first.wait()
    second.wait()

    def pieces():
        for cc in range(2):
            for yx in range(8):
                for s in range(8):
                    yield "c", cc, yx, 2 * yx, s, s
                yield "c", cc, yx, 2 * yx + 1, 6, 8
                for s in range(3):
                    yield "a", cc, yx, 2 * yx + 1, s, s
                    yield "b", cc, yx, 2 * yx + 1, s + 3, s

    def block(cc, at, slot):
        return wv[cc, at * 64 + slot * 8 : at * 64 + slot * 8 + 8, :]

    acc = {k: jnp.zeros((8, CH), F32) for k in "cab"}
    sq = {k: jnp.zeros((8, CH), F32) for k in "cab"}
    for kind, cc, yx, at, slot, _ in pieces():
        v = block(cc, at, slot)
        acc[kind] = acc[kind] + v
        sq[kind] = sq[kind] + v * v
    fan = {"c": CONV_FAN, "a": PROJ_FAN, "b": PROJ_FAN}
    mean = {k: jnp.sum(acc[k], axis=0, keepdims=True) * (1.0 / fan[k]) for k in "cab"}
    weight_sq = {k: jnp.sum(sq[k], axis=0, keepdims=True) for k in "cab"}
    spread = {k: jnp.zeros((8, CH), F32) for k in "cab"}
    for kind, cc, yx, at, slot, _ in pieces():
        v = block(cc, at, slot) - mean[kind]
        spread[kind] = spread[kind] + v * v
    spread = {k: jnp.sum(spread[k], axis=0, keepdims=True) for k in "cab"}
    factor = {k: lax.rsqrt(spread[k] + ws_eps) for k in "cab"}
    gain = {"c": cg_ref[...], "a": pg_ref[:, 0:CH], "b": pg_ref[:, CH:OUT]}
    scale = {k: gain[k] * factor[k] for k in "cab"}
    for n, stat in enumerate((mean, factor, spread, weight_sq)):
        sc_ref[n : n + 1, :] = stat["c"]
        sp_ref[n : n + 1, 0:CH] = stat["a"]
        sp_ref[n : n + 1, CH:OUT] = stat["b"]
    sc_ref[4:8, :] = jnp.zeros((4, CH), F32)
    sp_ref[4:8, :] = jnp.zeros((4, OUT), F32)
    for kind, cc, yx, at, slot, j in pieces():
        v = scale[kind] * (block(cc, at, slot) - mean[kind])
        for lt in range(3):
            piece = v[:, lt * GW : (lt + 1) * GW]
            if kind == "c":
                wc[lt, pl.ds((yx * 2 + cc) * 9 + j, 8, stride=144), :] = piece
            else:
                tile = lt if kind == "a" else lt + 3
                wp[tile, pl.ds((yx * 2 + cc) * 3 + j, 8, stride=48), :] = piece
    for g in range(3):
        wcb[g] = wc[g].astype(BF16)
    for n in range(6):
        wpb[:, n * GW : (n + 1) * GW] = wp[n].astype(BF16)

    px9 = 9 * COLS
    og_all = og9[...].reshape(px9, OUT)
    for g in range(3):
        lanes = slice(g * GW, (g + 1) * GW)
        pre = jnp.zeros((px9, GW), F32)
        for i in range(3):
            pre = pre + jnp.dot(
                acat[g, i : i + 9].reshape(px9, 3 * GW),
                wcb[g, i * 3 * GW : (i + 1) * 3 * GW, :],
                preferred_element_type=F32,
            )
        value, slope = gelu_parts(pre)
        hid[:, :, lanes] = value.astype(BF16).reshape(9, COLS, GW)
        hidden_grad = lax.dot_general(
            og_all, wpb[lanes, :], (((1,), (1,)), ((), ())), preferred_element_type=F32
        )
        pre_grad = (hidden_grad * slope).astype(BF16)
        pp[pl.ds(1 - h, 9), :, lanes] = pre_grad.reshape(9, COLS, GW)
    pp[9 * h] = zero_row

    px = ROWS * COLS
    og_own = og_ref[...].reshape(px, OUT)
    for g in range(3):
        lanes = slice(g * GW, (g + 1) * GW)
        part = lax.dot_general(
            hid[pl.ds(h, ROWS), :, lanes].reshape(px, GW), og_own,
            (((0,), (0,)), ((), ())), preferred_element_type=F32,
        )
        for n in range(6):
            gp[n, lanes, :] = part[:, n * GW : (n + 1) * GW]
        grad_own = pp[1 : 1 + ROWS, :, lanes].reshape(px, GW)
        for i in range(3):
            gc[g, i * 3 * GW : (i + 1) * 3 * GW, :] = lax.dot_general(
                acat[g, pl.ds(h + i, ROWS)].reshape(px, 3 * GW), grad_own,
                (((0,), (0,)), ((), ())), preferred_element_type=F32,
            )
    for kind, cc, yx, at, slot, j in pieces():
        rows = slice(at * 64 + slot * 8, at * 64 + slot * 8 + 8)
        for lt in range(3):
            if kind == "c":
                piece = gc[lt, pl.ds((yx * 2 + cc) * 9 + j, 8, stride=144), :]
            else:
                tile = lt if kind == "a" else lt + 3
                piece = gp[tile, pl.ds((yx * 2 + cc) * 3 + j, 8, stride=48), :]
            go[cc, rows, lt * GW : (lt + 1) * GW] = piece
    for cc in range(2):
        for yx in range(8):
            at = (2 * yx + 1) * 64 + 56
            go[cc, at : at + 8, :] = jnp.zeros((8, CH), F32)
    own_ref[...] = go[core]
    send_ref[...] = go[1 - core].astype(BF16)

    col10 = lax.broadcasted_iota(jnp.int32, (10 * COLS, GW), 0) % COLS
    for g in range(3):
        lanes = slice(g * GW, (g + 1) * GW)
        grad = pp[:, :, lanes].reshape(10 * COLS, GW).astype(F32)
        psh[0] = shifted(grad, 1, col10).astype(BF16)
        psh[1] = grad.astype(BF16)
        psh[2] = shifted(grad, -1, col10).astype(BF16)
        total = jnp.zeros((px, GW), F32)
        for i in range(3):
            for j in range(3):
                tap = 3 * i + j
                total = total + lax.dot_general(
                    psh[j, (2 - i) * COLS : (2 - i) * COLS + px, :],
                    wcb[g, tap * GW : (tap + 1) * GW, :],
                    (((1,), (1,)), ((), ())), preferred_element_type=F32,
                )
        slope = gelu_parts(x_ref[:, :, lanes].reshape(px, GW).astype(F32))[1]
        ig_ref[:, :, lanes] = (total * slope).astype(BF16).reshape(ROWS, COLS, GW)


def main_call(where, wa, wb, x, og, halo, conv_gain, proj_gain):
    vmem = pl.BlockSpec(memory_space=pltpu.VMEM)
    far = pl.BlockSpec(memory_space=pl.ANY)
    return pl.pallas_call(
        main_kernel,
        out_shape=(
            jax.ShapeDtypeStruct((ROWS, COLS, CH), BF16),
            jax.ShapeDtypeStruct((1024, CH), F32),
            jax.ShapeDtypeStruct((1024, CH), BF16),
            jax.ShapeDtypeStruct((8, CH), F32),
            jax.ShapeDtypeStruct((8, OUT), F32),
        ),
        in_specs=[pl.BlockSpec(memory_space=pltpu.SMEM), far, far] + [vmem] * 5,
        out_specs=(vmem,) * 5,
        scratch_shapes=[
            pltpu.VMEM((2, 1024, CH), F32),
            pltpu.VMEM((3, CONV_FAN, GW), F32),
            pltpu.VMEM((6, PROJ_FAN, GW), F32),
            pltpu.VMEM((3, CONV_FAN, GW), BF16),
            pltpu.VMEM((PROJ_FAN, OUT), BF16),
            pltpu.VMEM((11, COLS, CH), BF16),
            pltpu.VMEM((3, 11, COLS, 3 * GW), BF16),
            pltpu.VMEM((9, COLS, OUT), BF16),
            pltpu.VMEM((9, COLS, CH), BF16),
            pltpu.VMEM((10, COLS, CH), BF16),
            pltpu.VMEM((3, 10 * COLS, GW), BF16),
            pltpu.VMEM((3, CONV_FAN, GW), F32),
            pltpu.VMEM((6, PROJ_FAN, GW), F32),
            pltpu.VMEM((2, 1024, CH), F32),
            pltpu.SemaphoreType.DMA((2,)),
        ],
        compiler_params=pltpu.CompilerParams(vmem_limit_bytes=VMEM_LIMIT),
        name="block",
    )(where, wa, wb, x, og, halo, conv_gain, proj_gain)


def moments_kernel(where_ref, arr_ref, w_ref, sc_ref, sp_ref, msg_ref, blk_ref):
    first = where_ref[0] == 0
    z = where_ref[2]
    mean_c = sc_ref[0:1, :]
    mean_a = sp_ref[0:1, 0:CH]
    mean_b = sp_ref[0:1, CH:OUT]
    at = lax.broadcasted_iota(jnp.int32, (8, CH), 0)
    sums = []
    for slot in range(8):
        rows = slice(slot * 8, slot * 8 + 8)
        grad = arr_ref[0, rows, :].astype(F32)
        for k in range(1, 8):
            grad = grad + arr_ref[k, rows, :].astype(F32)
        grad = grad * (1.0 / 128.0)
        other = mean_a if slot < 3 else mean_b if slot < 6 else mean_c
        cent = w_ref[rows, :] - jnp.where(first, mean_c, other)
        sums.append((grad, grad * cent, grad * grad))
        blk_ref[slot : slot + 1, :] = jnp.sum(
            jnp.where(at == z, grad, 0.0), axis=0, keepdims=True
        )
    lines = []
    for n in range(3):
        part_a = sums[0][n] + sums[1][n] + sums[2][n]
        part_b = sums[3][n] + sums[4][n] + sums[5][n]
        part_c = sums[6][n] + sums[7][n]
        conv = part_c + jnp.where(first, part_a + part_b, 0.0)
        for part in (conv, jnp.where(first, 0.0, part_a), jnp.where(first, 0.0, part_b)):
            lines.append(jnp.sum(part, axis=0, keepdims=True))
    for peer in range(32):
        for n, line in enumerate(lines):
            for lt in range(3):
                msg_ref[peer, 3 * n + lt : 3 * n + lt + 1, :] = line[:, lt * GW : (lt + 1) * GW]
        msg_ref[peer, 27:32, :] = jnp.zeros((5, GW), F32)


def moments_call(where, arr, w_own, sc, sp):
    vmem = pl.BlockSpec(memory_space=pltpu.VMEM)
    return pl.pallas_call(
        moments_kernel,
        out_shape=(
            jax.ShapeDtypeStruct((32, 32, GW), F32),
            jax.ShapeDtypeStruct((8, CH), F32),
        ),
        in_specs=[pl.BlockSpec(memory_space=pltpu.SMEM)] + [vmem] * 4,
        out_specs=(vmem,) * 2,
        name="moments",
    )(where, arr, w_own, sc, sp)


def update_kernel(
    where_ref, stat_ref, own_ref, other_ref, cw_ref, cm_ref, pw_ref, pm_ref, sc_ref, sp_ref,
    cg_ref, pg_ref, ncw_ref, ncm_ref, npw_ref, npm_ref,
):
    first = where_ref[0] == 0
    total = stat_ref[0]
    for k in range(1, 32):
        total = total + stat_ref[k]

    def line(n):
        return jnp.concatenate([total[3 * n + lt : 3 * n + lt + 1, :] for lt in range(3)], axis=1)

    own = own_ref[...]
    other = other_ref[...]
    low = jnp.where(first, own, other)
    high = jnp.where(first, other, own)

    def update(weight, mom, grad, sums, stat, gain, fan):
        grad_sum, grad_proj, grad_square = sums
        mean, factor, spread, weight_sq = stat
        one = gain * factor
        two = gain * factor * factor * factor * grad_proj
        raw = one * (grad - grad_sum * (1.0 / fan)) - two * (weight - mean)
        square = (
            one * one * (grad_square - grad_sum * grad_sum * (1.0 / fan))
            - 2.0 * one * two * grad_proj
            + two * two * spread
        )
        square = jnp.maximum(square, 0.0)
        clip = jnp.minimum(1.0, clip_ratio * jnp.sqrt(weight_sq) * lax.rsqrt(square + norm_eps))
        clipped = raw * clip
        new = momentum_rate * mom + clipped
        return weight - learn_rate * (clipped + momentum_rate * new), new

    conv_sums = [line(3 * n) for n in range(3)]
    conv_stat = [sc_ref[n : n + 1, :] for n in range(4)]
    for rows, grad in ((slice(0, 8), low), (slice(8, 9), high[6:7, :])):
        weight, mom = update(
            cw_ref[rows, :], cm_ref[rows, :], grad, conv_sums, conv_stat, cg_ref[...], CONV_FAN
        )
        ncw_ref[rows, :] = weight
        ncm_ref[rows, :] = mom
    for part in range(2):
        lanes = slice(part * CH, (part + 1) * CH)
        weight, mom = update(
            pw_ref[:, lanes], pm_ref[:, lanes], high[3 * part : 3 * part + 3, :],
            [line(3 * n + 1 + part) for n in range(3)],
            [sp_ref[n : n + 1, lanes] for n in range(4)], pg_ref[:, lanes], PROJ_FAN,
        )
        npw_ref[:, lanes] = weight
        npm_ref[:, lanes] = mom


def update_call(*args):
    vmem = pl.BlockSpec(memory_space=pltpu.VMEM)
    return pl.pallas_call(
        update_kernel,
        out_shape=(
            jax.ShapeDtypeStruct((9, CH), F32),
            jax.ShapeDtypeStruct((9, CH), F32),
            jax.ShapeDtypeStruct((3, OUT), F32),
            jax.ShapeDtypeStruct((3, OUT), F32),
        ),
        in_specs=[pl.BlockSpec(memory_space=pltpu.SMEM)] + [vmem] * (len(args) - 1),
        out_specs=(vmem,) * 4,
        name="update",
    )(*args)


def swap(a, axis):
    return lax.ppermute(a, axis, [(0, 1), (1, 0)])


def copies(a, axis):
    n = lax.axis_size(axis)
    return lax.all_to_all(jnp.broadcast_to(a[None], (n, *a.shape)), axis, 0, 0, tiled=True)


def local(
    block_input, output_grad, conv_weight, conv_gain, conv_momentum, proj_weight, proj_gain,
    proj_momentum,
):
    h = lax.axis_index("rows")
    where = jnp.stack([h, lax.axis_index("core"), lax.axis_index("z")]).astype(jnp.int32)
    cw, cm, pw, pm = conv_weight.T, conv_momentum.T, proj_weight.T, proj_momentum.T
    cg, pg = conv_gain.reshape(1, CH), proj_gain.reshape(1, OUT)
    x, og = block_input[0], output_grad[0]

    low = cw[0:8]
    high = jnp.concatenate([pw[:, :CH], pw[:, CH:], cw[8:9], jnp.zeros((1, CH), F32)], axis=0)
    mine = jnp.where(h == 0, low, high)
    w_own = copies(mine, "z").swapaxes(0, 1).reshape(64, CH)

    edge_x = jnp.where(h == 0, x[ROWS - 2 :], x[:2])
    edge_og = jnp.where(h == 0, og[ROWS - 1], og[0])
    halo = swap(jnp.concatenate([edge_x, edge_og[None, :, :CH], edge_og[None, :, CH:]]), "rows")

    wa = copies(w_own, PLANE).reshape(1024, CH)
    wb = swap(wa, "core")
    input_grad, own, send, sc, sp = main_call(where, wa, wb, x, og, halo, cg, pg)

    pair = (own + swap(send, "core").astype(F32)).astype(BF16).reshape(16, 64, CH)
    plane = lax.all_to_all(pair, PLANE, 0, 0, tiled=True).astype(F32).sum(axis=0).astype(BF16)
    arr = copies(plane, "z")
    msg, blk = moments_call(where, arr, w_own, sc, sp)
    other = swap(blk, "rows")
    stat = lax.all_to_all(msg, ("y", "x", "core", "rows"), 0, 0, tiled=True)
    ncw, ncm, npw, npm = update_call(
        where, stat, blk, other, cw, cm, pw, pm, sc, sp, cg, pg
    )
    return input_grad[None], ncw.T, ncm.T, npw.T, npm.T


def solution(mesh):
    split = Mesh(
        mesh.devices.reshape(8, 4, 2, 2, mesh.shape["rows"]), ("z", "y", "x", "core", "rows")
    )
    maps = P(BATCH, "rows", None, None)
    columns = P(None, BATCH)
    return jax.shard_map(
        local,
        mesh=split,
        in_specs=(maps, maps, columns, P(), columns, columns, P(), columns),
        out_specs=(maps, columns, columns, columns, columns),
        check_vma=False,
    )
```

```python
import jax
import jax.numpy as jnp
from jax import lax
from jax.experimental import pallas as pl
from jax.experimental.pallas import tpu as pltpu
from jax.sharding import Mesh
from jax.sharding import PartitionSpec as P

CH = 384
GW = 128
OUT = 768
CONV_FAN = 9 * GW
PROJ_FAN = CH
ROWS = 8
COLS = 64
BATCH = ("z", "y", "x", "core")
PLANE = ("y", "x", "rows")

ws_eps = 0.0001
clip_ratio = 0.05
momentum_rate = 0.9
learn_rate = 1.6
norm_eps = 1e-06

F32 = jnp.float32
BF16 = jnp.bfloat16


def gelu_parts(v):
    k = 0.7978845608028654
    sq = v * v
    t = jnp.tanh(k * (v + 0.044715 * (v * sq)))
    half = 0.5 * (1.0 + t)
    slope = half + 0.5 * v * (1.0 - t * t) * (k * (1.0 + 3.0 * 0.044715 * sq))
    return v * half, slope


def shifted(v, step, col):
    n = v.shape[0]
    moved = pltpu.roll(v, (-step) % n, 0)
    edge = COLS - 1 if step > 0 else 0
    return jnp.where(col == edge, 0.0, moved)


def cost(flops, nbytes):
    return pl.CostEstimate(flops=flops, bytes_accessed=nbytes, transcendentals=0)


def small(nbytes=4 * 1024 * 1024):
    return pltpu.CompilerParams(vmem_limit_bytes=nbytes)


def pack_kernel(cw_hbm, pw_hbm, x_hbm, og_hbm, out_ref, edge_ref, cw_ref, pw_ref, sems):
    h = lax.axis_index("rows")
    last = 1 - h
    moves = [
        (cw_hbm, cw_ref),
        (pw_hbm, pw_ref),
        (x_hbm.at[pl.ds(last * (ROWS - 2), 2)], edge_ref.at[pl.ds(0, 2)]),
        (og_hbm.at[last * (ROWS - 1), :, pl.ds(0, CH)], edge_ref.at[2]),
        (og_hbm.at[last * (ROWS - 1), :, pl.ds(CH, CH)], edge_ref.at[3]),
    ]
    moves = [pltpu.make_async_copy(*m, sems.at[n]) for n, m in enumerate(moves)]
    for m in moves:
        m.start()
    moves[0].wait()
    moves[1].wait()
    low = cw_ref[0:8, :]
    high = jnp.concatenate(
        [pw_ref[:, 0:CH], pw_ref[:, CH:OUT], cw_ref[8:9, :], jnp.zeros((1, CH), F32)], axis=0
    )
    mine = jnp.where(h == 0, low, high)
    for k in range(8):
        out_ref[k] = mine
    for m in moves[2:]:
        m.wait()


def pack_call(cw, pw, x, og):
    vmem = pl.BlockSpec(memory_space=pltpu.VMEM)
    far = pl.BlockSpec(memory_space=pl.ANY)
    return pl.pallas_call(
        pack_kernel,
        out_shape=(
            jax.ShapeDtypeStruct((8, 8, CH), F32),
            jax.ShapeDtypeStruct((4, COLS, CH), BF16),
        ),
        in_specs=[far] * 4,
        out_specs=(vmem, vmem),
        scratch_shapes=[
            pltpu.VMEM((9, CH), F32),
            pltpu.VMEM((3, OUT), F32),
            pltpu.SemaphoreType.DMA((5,)),
        ],
        compiler_params=small(60 * 1024 * 1024),
        name="pack",
    )(cw, pw, x, og)


def patches_kernel(x_ref, halo_ref, acat_ref, xs):
    h = lax.axis_index("rows")
    xs[pl.ds(1 + h, ROWS)] = x_ref[...]
    zero_row = jnp.zeros((COLS, CH), BF16)

    @pl.when(h == 0)
    def _():
        xs[0] = zero_row
        xs[9] = halo_ref[0]
        xs[10] = halo_ref[1]

    @pl.when(h == 1)
    def _():
        xs[0] = halo_ref[0]
        xs[1] = halo_ref[1]
        xs[10] = zero_row

    col = lax.broadcasted_iota(jnp.int32, (11 * COLS, GW), 0) % COLS
    for g in range(3):
        lanes = slice(g * GW, (g + 1) * GW)
        act = gelu_parts(xs[:, :, lanes].reshape(11 * COLS, GW).astype(F32))[0]
        for j, piece in enumerate((shifted(act, -1, col), act, shifted(act, 1, col))):
            acat_ref[g, :, :, j * GW : (j + 1) * GW] = piece.astype(BF16).reshape(11, COLS, GW)


def patches_call(x, halo):
    vmem = pl.BlockSpec(memory_space=pltpu.VMEM)
    return pl.pallas_call(
        patches_kernel,
        out_shape=jax.ShapeDtypeStruct((3, 11, COLS, 3 * GW), BF16),
        in_specs=[vmem, vmem],
        out_specs=vmem,
        scratch_shapes=[pltpu.VMEM((11, COLS, CH), BF16)],
        compiler_params=pltpu.CompilerParams(vmem_limit_bytes=12 * 1024 * 1024),
        cost_estimate=cost(8 * 10**6, 2 * 10**6),
        name="patches",
    )(x, halo)


def main_kernel(
    wa_ref, wb_ref, acat, og_ref, halo_ref, cg_ref, pg_ref,
    own_ref, send_ref, sc_ref, sp_ref, wcb, pp,
    wv, wc, wp, wpb, og9, hid, sems,
):
    h = lax.axis_index("rows")
    core = lax.axis_index("core")
    first = pltpu.make_async_copy(wa_ref, wv.at[core], sems.at[0])
    second = pltpu.make_async_copy(wb_ref, wv.at[1 - core], sems.at[1])
    first.start()
    second.start()

    og9[pl.ds(h, ROWS)] = og_ref[...]
    at_halo = 8 * (1 - h)
    og9[at_halo, :, 0:CH] = halo_ref[2]
    og9[at_halo, :, CH:OUT] = halo_ref[3]
    zero_row = jnp.zeros((COLS, CH), BF16)
    first.wait()
    second.wait()

    def pieces():
        for cc in range(2):
            for yx in range(8):
                for s in range(8):
                    yield "c", cc, yx, 2 * yx, s, s
                yield "c", cc, yx, 2 * yx + 1, 6, 8
                for s in range(3):
                    yield "a", cc, yx, 2 * yx + 1, s, s
                    yield "b", cc, yx, 2 * yx + 1, s + 3, s

    def block(cc, at, slot):
        return wv[cc, at * 64 + slot * 8 : at * 64 + slot * 8 + 8, :]

    acc = {k: jnp.zeros((8, CH), F32) for k in "cab"}
    sq = {k: jnp.zeros((8, CH), F32) for k in "cab"}
    for kind, cc, yx, at, slot, _ in pieces():
        v = block(cc, at, slot)
        acc[kind] = acc[kind] + v
        sq[kind] = sq[kind] + v * v
    fan = {"c": CONV_FAN, "a": PROJ_FAN, "b": PROJ_FAN}
    mean = {k: jnp.sum(acc[k], axis=0, keepdims=True) * (1.0 / fan[k]) for k in "cab"}
    weight_sq = {k: jnp.sum(sq[k], axis=0, keepdims=True) for k in "cab"}
    spread = {k: jnp.zeros((8, CH), F32) for k in "cab"}
    for kind, cc, yx, at, slot, _ in pieces():
        v = block(cc, at, slot) - mean[kind]
        spread[kind] = spread[kind] + v * v
    spread = {k: jnp.sum(spread[k], axis=0, keepdims=True) for k in "cab"}
    factor = {k: lax.rsqrt(spread[k] + ws_eps) for k in "cab"}
    gain = {"c": cg_ref[...], "a": pg_ref[:, 0:CH], "b": pg_ref[:, CH:OUT]}
    scale = {k: gain[k] * factor[k] for k in "cab"}
    for n, stat in enumerate((mean, factor, spread, weight_sq)):
        sc_ref[n : n + 1, :] = stat["c"]
        sp_ref[n : n + 1, 0:CH] = stat["a"]
        sp_ref[n : n + 1, CH:OUT] = stat["b"]
    sc_ref[4:8, :] = jnp.zeros((4, CH), F32)
    sp_ref[4:8, :] = jnp.zeros((4, OUT), F32)
    for kind, cc, yx, at, slot, j in pieces():
        v = scale[kind] * (block(cc, at, slot) - mean[kind])
        for lt in range(3):
            piece = v[:, lt * GW : (lt + 1) * GW]
            if kind == "c":
                wc[lt, pl.ds((yx * 2 + cc) * 9 + j, 8, stride=144), :] = piece
            else:
                tile = lt if kind == "a" else lt + 3
                wp[tile, pl.ds((yx * 2 + cc) * 3 + j, 8, stride=48), :] = piece
    for g in range(3):
        wcb[g] = wc[g].astype(BF16)
    for n in range(6):
        wpb[:, n * GW : (n + 1) * GW] = wp[n].astype(BF16)

    px9 = 9 * COLS
    og_all = og9[...].reshape(px9, OUT)
    for g in range(3):
        lanes = slice(g * GW, (g + 1) * GW)
        pre = jnp.zeros((px9, GW), F32)
        for i in range(3):
            pre = pre + jnp.dot(
                acat[g, i : i + 9].reshape(px9, 3 * GW),
                wcb[g, i * 3 * GW : (i + 1) * 3 * GW, :],
                preferred_element_type=F32,
            )
        value, slope = gelu_parts(pre)
        hid[:, :, lanes] = value.astype(BF16).reshape(9, COLS, GW)
        hidden_grad = lax.dot_general(
            og_all, wpb[lanes, :], (((1,), (1,)), ((), ())), preferred_element_type=F32
        )
        pre_grad = (hidden_grad * slope).astype(BF16)
        pp[pl.ds(1 - h, 9), :, lanes] = pre_grad.reshape(9, COLS, GW)
    pp[9 * h] = zero_row

    px = ROWS * COLS
    og_own = og_ref[...].reshape(px, OUT)
    for g in range(3):
        lanes = slice(g * GW, (g + 1) * GW)
        part = lax.dot_general(
            hid[pl.ds(h, ROWS), :, lanes].reshape(px, GW), og_own,
            (((0,), (0,)), ((), ())), preferred_element_type=F32,
        )
        for n in range(6):
            wp[n, lanes, :] = part[:, n * GW : (n + 1) * GW]
        grad_own = pp[1 : 1 + ROWS, :, lanes].reshape(px, GW)
        for i in range(3):
            wc[g, i * 3 * GW : (i + 1) * 3 * GW, :] = lax.dot_general(
                acat[g, pl.ds(h + i, ROWS)].reshape(px, 3 * GW), grad_own,
                (((0,), (0,)), ((), ())), preferred_element_type=F32,
            )
    for kind, cc, yx, at, slot, j in pieces():
        rows = slice(at * 64 + slot * 8, at * 64 + slot * 8 + 8)
        for lt in range(3):
            if kind == "c":
                piece = wc[lt, pl.ds((yx * 2 + cc) * 9 + j, 8, stride=144), :]
            else:
                tile = lt if kind == "a" else lt + 3
                piece = wp[tile, pl.ds((yx * 2 + cc) * 3 + j, 8, stride=48), :]
            wv[cc, rows, lt * GW : (lt + 1) * GW] = piece
    for cc in range(2):
        for yx in range(8):
            at = (2 * yx + 1) * 64 + 56
            wv[cc, at : at + 8, :] = jnp.zeros((8, CH), F32)
    own_ref[...] = wv[core]
    send_ref[...] = wv[1 - core].astype(BF16)


def main_call(wa, wb, acat, og, halo, conv_gain, proj_gain):
    vmem = pl.BlockSpec(memory_space=pltpu.VMEM)
    far = pl.BlockSpec(memory_space=pl.ANY)
    return pl.pallas_call(
        main_kernel,
        out_shape=(
            jax.ShapeDtypeStruct((1024, CH), F32),
            jax.ShapeDtypeStruct((1024, CH), BF16),
            jax.ShapeDtypeStruct((8, CH), F32),
            jax.ShapeDtypeStruct((8, OUT), F32),
            jax.ShapeDtypeStruct((3, CONV_FAN, GW), BF16),
            jax.ShapeDtypeStruct((10, COLS, CH), BF16),
        ),
        in_specs=[far, far] + [vmem] * 5,
        out_specs=(vmem,) * 6,
        scratch_shapes=[
            pltpu.VMEM((2, 1024, CH), F32),
            pltpu.VMEM((3, CONV_FAN, GW), F32),
            pltpu.VMEM((6, PROJ_FAN, GW), F32),
            pltpu.VMEM((PROJ_FAN, OUT), BF16),
            pltpu.VMEM((9, COLS, OUT), BF16),
            pltpu.VMEM((9, COLS, CH), BF16),
            pltpu.SemaphoreType.DMA((2,)),
        ],
        compiler_params=pltpu.CompilerParams(vmem_limit_bytes=32 * 1024 * 1024),
        cost_estimate=cost(15 * 10**8, 10**7),
        name="block",
    )(wa, wb, acat, og, halo, conv_gain, proj_gain)


def input_kernel(x_ref, wcb, pp, ig_ref, psh):
    px = ROWS * COLS
    col = lax.broadcasted_iota(jnp.int32, (10 * COLS, GW), 0) % COLS
    for g in range(3):
        lanes = slice(g * GW, (g + 1) * GW)
        grad = pp[:, :, lanes].reshape(10 * COLS, GW).astype(F32)
        psh[0] = shifted(grad, 1, col).astype(BF16)
        psh[1] = grad.astype(BF16)
        psh[2] = shifted(grad, -1, col).astype(BF16)
        total = jnp.zeros((px, GW), F32)
        for i in range(3):
            for j in range(3):
                tap = 3 * i + j
                total = total + lax.dot_general(
                    psh[j, (2 - i) * COLS : (2 - i) * COLS + px, :],
                    wcb[g, tap * GW : (tap + 1) * GW, :],
                    (((1,), (1,)), ((), ())), preferred_element_type=F32,
                )
        slope = gelu_parts(x_ref[:, :, lanes].reshape(px, GW).astype(F32))[1]
        ig_ref[:, :, lanes] = (total * slope).astype(BF16).reshape(ROWS, COLS, GW)


def input_call(x, wcb, pp):
    vmem = pl.BlockSpec(memory_space=pltpu.VMEM)
    return pl.pallas_call(
        input_kernel,
        out_shape=jax.ShapeDtypeStruct((ROWS, COLS, CH), BF16),
        in_specs=[vmem] * 3,
        out_specs=vmem,
        scratch_shapes=[pltpu.VMEM((3, 10 * COLS, GW), BF16)],
        compiler_params=pltpu.CompilerParams(vmem_limit_bytes=12 * 1024 * 1024),
        cost_estimate=cost(5 * 10**8, 3 * 10**6),
        name="input_gradient",
    )(x, wcb, pp)


def moments_kernel(arr_ref, w_ref, sc_ref, sp_ref, msg_ref, blk_ref, line_ref):
    first = lax.axis_index("rows") == 0
    z = lax.axis_index("z")
    mean_c = sc_ref[0:1, :]
    mean_a = sp_ref[0:1, 0:CH]
    mean_b = sp_ref[0:1, CH:OUT]
    at = lax.broadcasted_iota(jnp.int32, (8, CH), 0)
    sums = []
    for slot in range(8):
        rows = slice(slot * 8, slot * 8 + 8)
        grad = arr_ref[0, rows, :].astype(F32)
        for k in range(1, 8):
            grad = grad + arr_ref[k, rows, :].astype(F32)
        grad = grad * (1.0 / 128.0)
        other = mean_a if slot < 3 else mean_b if slot < 6 else mean_c
        cent = w_ref[rows, :] - jnp.where(first, mean_c, other)
        sums.append((grad, grad * cent, grad * grad))
        blk_ref[slot : slot + 1, :] = jnp.sum(
            jnp.where(at == z, grad, 0.0), axis=0, keepdims=True
        )
    lines = []
    for n in range(3):
        part_a = sums[0][n] + sums[1][n] + sums[2][n]
        part_b = sums[3][n] + sums[4][n] + sums[5][n]
        part_c = sums[6][n] + sums[7][n]
        conv = part_c + jnp.where(first, part_a + part_b, 0.0)
        for part in (conv, jnp.where(first, 0.0, part_a), jnp.where(first, 0.0, part_b)):
            lines.append(jnp.sum(part, axis=0, keepdims=True))
    for n, line in enumerate(lines):
        for lt in range(3):
            line_ref[3 * n + lt : 3 * n + lt + 1, :] = line[:, lt * GW : (lt + 1) * GW]
    line_ref[27:32, :] = jnp.zeros((5, GW), F32)
    message = line_ref[...]
    for peer in range(32):
        msg_ref[peer] = message


def moments_call(arr, w_own, sc, sp):
    vmem = pl.BlockSpec(memory_space=pltpu.VMEM)
    return pl.pallas_call(
        moments_kernel,
        out_shape=(
            jax.ShapeDtypeStruct((32, 32, GW), F32),
            jax.ShapeDtypeStruct((8, CH), F32),
        ),
        in_specs=[vmem] * 4,
        out_specs=(vmem,) * 2,
        scratch_shapes=[pltpu.VMEM((32, GW), F32)],
        compiler_params=small(),
        name="moments",
    )(arr, w_own, sc, sp)


def update_kernel(
    stat_ref, own_ref, other_ref, cw_ref, cm_ref, pw_ref, pm_ref, sc_ref, sp_ref,
    cg_ref, pg_ref, ncw_ref, ncm_ref, npw_ref, npm_ref,
):
    first = lax.axis_index("rows") == 0
    total = stat_ref[0]
    for k in range(1, 32):
        total = total + stat_ref[k]

    def line(n):
        return jnp.concatenate([total[3 * n + lt : 3 * n + lt + 1, :] for lt in range(3)], axis=1)

    own = own_ref[...]
    other = other_ref[...]
    low = jnp.where(first, own, other)
    high = jnp.where(first, other, own)

    def update(weight, mom, grad, sums, stat, gain, fan):
        grad_sum, grad_proj, grad_square = sums
        mean, factor, spread, weight_sq = stat
        one = gain * factor
        two = gain * factor * factor * factor * grad_proj
        raw = one * (grad - grad_sum * (1.0 / fan)) - two * (weight - mean)
        square = (
            one * one * (grad_square - grad_sum * grad_sum * (1.0 / fan))
            - 2.0 * one * two * grad_proj
            + two * two * spread
        )
        square = jnp.maximum(square, 0.0)
        clip = jnp.minimum(1.0, clip_ratio * jnp.sqrt(weight_sq) * lax.rsqrt(square + norm_eps))
        clipped = raw * clip
        new = momentum_rate * mom + clipped
        return weight - learn_rate * (clipped + momentum_rate * new), new

    conv_sums = [line(3 * n) for n in range(3)]
    conv_stat = [sc_ref[n : n + 1, :] for n in range(4)]
    for rows, grad in ((slice(0, 8), low), (slice(8, 9), high[6:7, :])):
        weight, mom = update(
            cw_ref[rows, :], cm_ref[rows, :], grad, conv_sums, conv_stat, cg_ref[...], CONV_FAN
        )
        ncw_ref[rows, :] = weight
        ncm_ref[rows, :] = mom
    for part in range(2):
        lanes = slice(part * CH, (part + 1) * CH)
        weight, mom = update(
            pw_ref[:, lanes], pm_ref[:, lanes], high[3 * part : 3 * part + 3, :],
            [line(3 * n + 1 + part) for n in range(3)],
            [sp_ref[n : n + 1, lanes] for n in range(4)], pg_ref[:, lanes], PROJ_FAN,
        )
        npw_ref[:, lanes] = weight
        npm_ref[:, lanes] = mom


def update_call(*args):
    vmem = pl.BlockSpec(memory_space=pltpu.VMEM)
    return pl.pallas_call(
        update_kernel,
        out_shape=(
            jax.ShapeDtypeStruct((9, CH), F32),
            jax.ShapeDtypeStruct((9, CH), F32),
            jax.ShapeDtypeStruct((3, OUT), F32),
            jax.ShapeDtypeStruct((3, OUT), F32),
        ),
        in_specs=[vmem] * len(args),
        out_specs=(vmem,) * 4,
        compiler_params=small(),
        name="update",
    )(*args)


def swap(a, axis):
    return lax.ppermute(a, axis, [(0, 1), (1, 0)])


def copies(a, axis):
    n = lax.axis_size(axis)
    return lax.all_to_all(jnp.broadcast_to(a[None], (n, *a.shape)), axis, 0, 0, tiled=True)


def local(
    block_input, output_grad, conv_weight, conv_gain, conv_momentum, proj_weight, proj_gain,
    proj_momentum,
):
    cw, cm, pw, pm = conv_weight.T, conv_momentum.T, proj_weight.T, proj_momentum.T
    cg, pg = conv_gain.reshape(1, CH), proj_gain.reshape(1, OUT)
    x, og = block_input[0], output_grad[0]

    mine, edge = pack_call(cw, pw, x, og)
    halo = swap(edge, "rows")
    w_own = lax.all_to_all(mine, "z", 0, 0, tiled=True)
    w_own, halo = lax.optimization_barrier((w_own, halo))
    w_own = w_own.swapaxes(0, 1).reshape(64, CH)
    wa = copies(w_own, PLANE).reshape(1024, CH)
    wb = swap(wa, "core")
    acat = patches_call(x, halo)
    own, send, sc, sp, wcb, pp = main_call(wa, wb, acat, og, halo, cg, pg)

    pair = (own + swap(send, "core").astype(F32)).astype(BF16).reshape(16, 64, CH)
    pair, pp = lax.optimization_barrier((pair, pp))
    input_grad = input_call(x, wcb, pp)
    plane = lax.all_to_all(pair, PLANE, 0, 0, tiled=True).astype(F32).sum(axis=0).astype(BF16)
    arr = copies(plane, "z")
    msg, blk = moments_call(arr, w_own, sc, sp)
    other = swap(blk, "rows")
    stat = lax.all_to_all(msg, ("y", "x", "core", "rows"), 0, 0, tiled=True)
    ncw, ncm, npw, npm = update_call(
        stat, blk, other, cw, cm, pw, pm, sc, sp, cg, pg
    )
    return input_grad[None], ncw.T, ncm.T, npw.T, npm.T


def solution(mesh):
    split = Mesh(
        mesh.devices.reshape(8, 4, 2, 2, mesh.shape["rows"]), ("z", "y", "x", "core", "rows")
    )
    maps = P(BATCH, "rows", None, None)
    columns = P(None, BATCH)
    return jax.shard_map(
        local,
        mesh=split,
        in_specs=(maps, maps, columns, P(), columns, columns, P(), columns),
        out_specs=(maps, columns, columns, columns, columns),
        check_vma=False,
    )
```

```python
import jax
import jax.numpy as jnp
from jax import lax
from jax.experimental import pallas as pl
from jax.experimental.pallas import tpu as pltpu
from jax.sharding import Mesh
from jax.sharding import PartitionSpec as P

CH = 384
GW = 128
OUT = 768
CONV_FAN = 9 * GW
PROJ_FAN = CH
ROWS = 8
COLS = 64
BATCH = ("z", "y", "x", "core")
PLANE = ("y", "x", "rows")

ws_eps = 0.0001
clip_ratio = 0.05
momentum_rate = 0.9
learn_rate = 1.6
norm_eps = 1e-06

F32 = jnp.float32
BF16 = jnp.bfloat16


def gelu_parts(v):
    k = 0.7978845608028654
    sq = v * v
    t = jnp.tanh(k * (v + 0.044715 * (v * sq)))
    half = 0.5 * (1.0 + t)
    slope = half + 0.5 * v * (1.0 - t * t) * (k * (1.0 + 3.0 * 0.044715 * sq))
    return v * half, slope


def shifted(v, step, col):
    n = v.shape[0]
    moved = pltpu.roll(v, (-step) % n, 0)
    edge = COLS - 1 if step > 0 else 0
    return jnp.where(col == edge, 0.0, moved)


def cost(flops, nbytes):
    return pl.CostEstimate(flops=flops, bytes_accessed=nbytes, transcendentals=0)


def small(nbytes=4 * 1024 * 1024):
    return pltpu.CompilerParams(vmem_limit_bytes=nbytes)


def pack_kernel(cw_hbm, pw_hbm, x_hbm, og_hbm, out_ref, edge_ref, cw_ref, pw_ref, sems):
    h = lax.axis_index("rows")
    last = 1 - h
    moves = [
        (cw_hbm, cw_ref),
        (pw_hbm, pw_ref),
        (x_hbm.at[pl.ds(last * (ROWS - 2), 2)], edge_ref.at[pl.ds(0, 2)]),
        (og_hbm.at[last * (ROWS - 1), :, pl.ds(0, CH)], edge_ref.at[2]),
        (og_hbm.at[last * (ROWS - 1), :, pl.ds(CH, CH)], edge_ref.at[3]),
    ]
    moves = [pltpu.make_async_copy(*m, sems.at[n]) for n, m in enumerate(moves)]
    for m in moves:
        m.start()
    moves[0].wait()
    moves[1].wait()
    low = jnp.concatenate([cw_ref[0:5, :], pw_ref[:, 0:CH]], axis=0)
    high = jnp.concatenate([cw_ref[5:9, :], jnp.zeros((1, CH), F32), pw_ref[:, CH:OUT]], axis=0)
    mine = jnp.where(h == 0, low, high)
    for k in range(8):
        out_ref[k] = mine
    for m in moves[2:]:
        m.wait()


def pack_call(cw, pw, x, og):
    vmem = pl.BlockSpec(memory_space=pltpu.VMEM)
    far = pl.BlockSpec(memory_space=pl.ANY)
    return pl.pallas_call(
        pack_kernel,
        out_shape=(
            jax.ShapeDtypeStruct((8, 8, CH), F32),
            jax.ShapeDtypeStruct((4, COLS, CH), BF16),
        ),
        in_specs=[far] * 4,
        out_specs=(vmem, vmem),
        scratch_shapes=[
            pltpu.VMEM((9, CH), F32),
            pltpu.VMEM((3, OUT), F32),
            pltpu.SemaphoreType.DMA((5,)),
        ],
        compiler_params=small(60 * 1024 * 1024),
        name="pack",
    )(cw, pw, x, og)


def patches_kernel(x_ref, halo_ref, acat_ref, xs):
    h = lax.axis_index("rows")
    xs[pl.ds(1 + h, ROWS)] = x_ref[...]
    zero_row = jnp.zeros((COLS, CH), BF16)

    @pl.when(h == 0)
    def _():
        xs[0] = zero_row
        xs[9] = halo_ref[0]
        xs[10] = halo_ref[1]

    @pl.when(h == 1)
    def _():
        xs[0] = halo_ref[0]
        xs[1] = halo_ref[1]
        xs[10] = zero_row

    col = lax.broadcasted_iota(jnp.int32, (11 * COLS, GW), 0) % COLS
    for g in range(3):
        lanes = slice(g * GW, (g + 1) * GW)
        act = gelu_parts(xs[:, :, lanes].reshape(11 * COLS, GW).astype(F32))[0]
        for j, piece in enumerate((shifted(act, -1, col), act, shifted(act, 1, col))):
            acat_ref[g, :, :, j * GW : (j + 1) * GW] = piece.astype(BF16).reshape(11, COLS, GW)


def patches_call(x, halo):
    vmem = pl.BlockSpec(memory_space=pltpu.VMEM)
    return pl.pallas_call(
        patches_kernel,
        out_shape=jax.ShapeDtypeStruct((3, 11, COLS, 3 * GW), BF16),
        in_specs=[vmem, vmem],
        out_specs=vmem,
        scratch_shapes=[pltpu.VMEM((11, COLS, CH), BF16)],
        compiler_params=pltpu.CompilerParams(vmem_limit_bytes=12 * 1024 * 1024),
        cost_estimate=cost(8 * 10**6, 2 * 10**6),
        name="patches",
    )(x, halo)


def main_kernel(
    wa_ref, wb_ref, acat, og_ref, halo_ref, cg_ref, pg_ref,
    own_ref, send_ref, sc_ref, sp_ref, wcb, pp,
    wc, wp, wpb, og9, hid,
):
    h = lax.axis_index("rows")
    core = lax.axis_index("core")

    og9[pl.ds(h, ROWS)] = og_ref[...]
    at_halo = 8 * (1 - h)
    og9[at_halo, :, 0:CH] = halo_ref[2]
    og9[at_halo, :, CH:OUT] = halo_ref[3]
    zero_row = jnp.zeros((COLS, CH), BF16)

    halves = (wa_ref, wb_ref)
    grads = (own_ref, send_ref)
    cores = (core, 1 - core)

    def pieces():
        for part in range(2):
            for yx in range(8):
                for s in range(5):
                    yield "c", part, yx, 2 * yx, s, s
                for s in range(4):
                    yield "c", part, yx, 2 * yx + 1, s, 5 + s
                for s in range(3):
                    yield "a", part, yx, 2 * yx, 5 + s, s
                    yield "b", part, yx, 2 * yx + 1, 5 + s, s

    def block(part, at, slot):
        return halves[part][at * 64 + slot * 8 : at * 64 + slot * 8 + 8, :]

    def strided(part, yx, kind, j):
        wide, apart = (9, 144) if kind == "c" else (3, 48)
        return pl.ds((yx * 2 + cores[part]) * wide + j, 8, stride=apart)

    acc = {k: jnp.zeros((8, CH), F32) for k in "cab"}
    sq = {k: jnp.zeros((8, CH), F32) for k in "cab"}
    for kind, part, yx, at, slot, _ in pieces():
        v = block(part, at, slot)
        acc[kind] = acc[kind] + v
        sq[kind] = sq[kind] + v * v
    fan = {"c": CONV_FAN, "a": PROJ_FAN, "b": PROJ_FAN}
    mean = {k: jnp.sum(acc[k], axis=0, keepdims=True) * (1.0 / fan[k]) for k in "cab"}
    weight_sq = {k: jnp.sum(sq[k], axis=0, keepdims=True) for k in "cab"}
    spread = {k: jnp.zeros((8, CH), F32) for k in "cab"}
    for kind, part, yx, at, slot, _ in pieces():
        v = block(part, at, slot) - mean[kind]
        spread[kind] = spread[kind] + v * v
    spread = {k: jnp.sum(spread[k], axis=0, keepdims=True) for k in "cab"}
    factor = {k: lax.rsqrt(spread[k] + ws_eps) for k in "cab"}
    gain = {"c": cg_ref[...], "a": pg_ref[:, 0:CH], "b": pg_ref[:, CH:OUT]}
    scale = {k: gain[k] * factor[k] for k in "cab"}
    for n, stat in enumerate((mean, factor, spread, weight_sq)):
        sc_ref[n : n + 1, :] = stat["c"]
        sp_ref[n : n + 1, 0:CH] = stat["a"]
        sp_ref[n : n + 1, CH:OUT] = stat["b"]
    sc_ref[4:8, :] = jnp.zeros((4, CH), F32)
    sp_ref[4:8, :] = jnp.zeros((4, OUT), F32)
    for kind, part, yx, at, slot, j in pieces():
        v = scale[kind] * (block(part, at, slot) - mean[kind])
        for lt in range(3):
            piece = v[:, lt * GW : (lt + 1) * GW]
            if kind == "c":
                wc[lt, strided(part, yx, kind, j), :] = piece
            else:
                wp[lt if kind == "a" else lt + 3, strided(part, yx, kind, j), :] = piece
    for g in range(3):
        wcb[g] = wc[g].astype(BF16)
    for n in range(6):
        wpb[:, n * GW : (n + 1) * GW] = wp[n].astype(BF16)

    px9 = 9 * COLS
    og_all = og9[...].reshape(px9, OUT)
    for g in range(3):
        lanes = slice(g * GW, (g + 1) * GW)
        pre = jnp.zeros((px9, GW), F32)
        for i in range(3):
            pre = pre + jnp.dot(
                acat[g, i : i + 9].reshape(px9, 3 * GW),
                wcb[g, i * 3 * GW : (i + 1) * 3 * GW, :],
                preferred_element_type=F32,
            )
        value, slope = gelu_parts(pre)
        hid[:, :, lanes] = value.astype(BF16).reshape(9, COLS, GW)
        hidden_grad = lax.dot_general(
            og_all, wpb[lanes, :], (((1,), (1,)), ((), ())), preferred_element_type=F32
        )
        pre_grad = (hidden_grad * slope).astype(BF16)
        pp[pl.ds(1 - h, 9), :, lanes] = pre_grad.reshape(9, COLS, GW)
    pp[9 * h] = zero_row

    px = ROWS * COLS
    og_own = og_ref[...].reshape(px, OUT)
    for g in range(3):
        lanes = slice(g * GW, (g + 1) * GW)
        part = lax.dot_general(
            hid[pl.ds(h, ROWS), :, lanes].reshape(px, GW), og_own,
            (((0,), (0,)), ((), ())), preferred_element_type=F32,
        )
        for n in range(6):
            wp[n, lanes, :] = part[:, n * GW : (n + 1) * GW]
        grad_own = pp[1 : 1 + ROWS, :, lanes].reshape(px, GW)
        for i in range(3):
            wc[g, i * 3 * GW : (i + 1) * 3 * GW, :] = lax.dot_general(
                acat[g, pl.ds(h + i, ROWS)].reshape(px, 3 * GW), grad_own,
                (((0,), (0,)), ((), ())), preferred_element_type=F32,
            )
    zero_block = jnp.zeros((8, GW), F32)
    for part in range(2):
        for at in range(16):
            for lt in range(3):
                found = []
                for slot in range(8):
                    kind, j = ("c", slot + 5 * (at % 2)) if slot < 5 else ("p", slot - 5)
                    if j == 9:
                        found.append(zero_block)
                    elif kind == "c":
                        found.append(wc[lt, strided(part, at // 2, kind, j), :])
                    else:
                        found.append(wp[lt + 3 * (at % 2), strided(part, at // 2, kind, j), :])
                for slot in range(0, 8, 2):
                    rows = slice(at * 64 + slot * 8, at * 64 + slot * 8 + 16)
                    pair = jnp.concatenate(found[slot : slot + 2], axis=0)
                    grads[part][rows, lt * GW : (lt + 1) * GW] = pair.astype(grads[part].dtype)


def main_call(wa, wb, acat, og, halo, conv_gain, proj_gain):
    vmem = pl.BlockSpec(memory_space=pltpu.VMEM)
    return pl.pallas_call(
        main_kernel,
        out_shape=(
            jax.ShapeDtypeStruct((1024, CH), F32),
            jax.ShapeDtypeStruct((1024, CH), BF16),
            jax.ShapeDtypeStruct((8, CH), F32),
            jax.ShapeDtypeStruct((8, OUT), F32),
            jax.ShapeDtypeStruct((3, CONV_FAN, GW), BF16),
            jax.ShapeDtypeStruct((10, COLS, CH), BF16),
        ),
        in_specs=[vmem] * 7,
        out_specs=(vmem,) * 6,
        scratch_shapes=[
            pltpu.VMEM((3, CONV_FAN, GW), F32),
            pltpu.VMEM((6, PROJ_FAN, GW), F32),
            pltpu.VMEM((PROJ_FAN, OUT), BF16),
            pltpu.VMEM((9, COLS, OUT), BF16),
            pltpu.VMEM((9, COLS, CH), BF16),
        ],
        compiler_params=pltpu.CompilerParams(vmem_limit_bytes=32 * 1024 * 1024),
        cost_estimate=cost(15 * 10**8, 10**7),
        name="block",
    )(wa, wb, acat, og, halo, conv_gain, proj_gain)


def input_kernel(x_ref, wcb, pp, ig_ref, psh):
    px = ROWS * COLS
    col = lax.broadcasted_iota(jnp.int32, (10 * COLS, GW), 0) % COLS
    for g in range(3):
        lanes = slice(g * GW, (g + 1) * GW)
        grad = pp[:, :, lanes].reshape(10 * COLS, GW).astype(F32)
        psh[0] = shifted(grad, 1, col).astype(BF16)
        psh[1] = grad.astype(BF16)
        psh[2] = shifted(grad, -1, col).astype(BF16)
        total = jnp.zeros((px, GW), F32)
        for i in range(3):
            for j in range(3):
                tap = 3 * i + j
                total = total + lax.dot_general(
                    psh[j, (2 - i) * COLS : (2 - i) * COLS + px, :],
                    wcb[g, tap * GW : (tap + 1) * GW, :],
                    (((1,), (1,)), ((), ())), preferred_element_type=F32,
                )
        slope = gelu_parts(x_ref[:, :, lanes].reshape(px, GW).astype(F32))[1]
        ig_ref[:, :, lanes] = (total * slope).astype(BF16).reshape(ROWS, COLS, GW)


def input_call(x, wcb, pp):
    vmem = pl.BlockSpec(memory_space=pltpu.VMEM)
    return pl.pallas_call(
        input_kernel,
        out_shape=jax.ShapeDtypeStruct((ROWS, COLS, CH), BF16),
        in_specs=[vmem] * 3,
        out_specs=vmem,
        scratch_shapes=[pltpu.VMEM((3, 10 * COLS, GW), BF16)],
        compiler_params=pltpu.CompilerParams(vmem_limit_bytes=12 * 1024 * 1024),
        cost_estimate=cost(5 * 10**8, 3 * 10**6),
        name="input_gradient",
    )(x, wcb, pp)


def moments_kernel(arr_ref, w_ref, sc_ref, sp_ref, msg_ref, blk_ref, line_ref):
    first = lax.axis_index("rows") == 0
    z = lax.axis_index("z")
    mean_c = sc_ref[0:1, :]
    mean_p = jnp.where(first, sp_ref[0:1, 0:CH], sp_ref[0:1, CH:OUT])
    at = lax.broadcasted_iota(jnp.int32, (8, CH), 0)
    sums = []
    for slot in range(8):
        rows = slice(slot * 8, slot * 8 + 8)
        grad = arr_ref[0, rows, :].astype(F32)
        for k in range(1, 8):
            grad = grad + arr_ref[k, rows, :].astype(F32)
        grad = grad * (1.0 / 128.0)
        cent = w_ref[rows, :] - (mean_c if slot < 5 else mean_p)
        sums.append((grad, grad * cent, grad * grad))
        blk_ref[slot : slot + 1, :] = jnp.sum(
            jnp.where(at == z, grad, 0.0), axis=0, keepdims=True
        )
    lines = []
    for n in range(3):
        conv = sums[0][n] + sums[1][n] + sums[2][n] + sums[3][n] + sums[4][n]
        proj = sums[5][n] + sums[6][n] + sums[7][n]
        lines.append(jnp.sum(conv, axis=0, keepdims=True))
        lines.append(jnp.sum(proj, axis=0, keepdims=True))
    for n, line in enumerate(lines):
        for lt in range(3):
            line_ref[3 * n + lt : 3 * n + lt + 1, :] = line[:, lt * GW : (lt + 1) * GW]
    line_ref[18:24, :] = jnp.zeros((6, GW), F32)
    message = line_ref[...]
    for peer in range(32):
        msg_ref[peer] = message


def moments_call(arr, w_own, sc, sp):
    vmem = pl.BlockSpec(memory_space=pltpu.VMEM)
    return pl.pallas_call(
        moments_kernel,
        out_shape=(
            jax.ShapeDtypeStruct((32, 24, GW), F32),
            jax.ShapeDtypeStruct((8, CH), F32),
        ),
        in_specs=[vmem] * 4,
        out_specs=(vmem,) * 2,
        scratch_shapes=[pltpu.VMEM((24, GW), F32)],
        compiler_params=small(),
        name="moments",
    )(arr, w_own, sc, sp)


def update_kernel(
    stat_ref, own_ref, other_ref, cw_ref, cm_ref, pw_ref, pm_ref, sc_ref, sp_ref,
    cg_ref, pg_ref, ncw_ref, ncm_ref, npw_ref, npm_ref,
):
    first = lax.axis_index("rows") == 0
    from_low, from_high = stat_ref[0], stat_ref[1]
    for k in range(2, 32, 2):
        from_low = from_low + stat_ref[k]
        from_high = from_high + stat_ref[k + 1]
    from_both = from_low + from_high

    def line(total, n):
        return jnp.concatenate([total[3 * n + lt : 3 * n + lt + 1, :] for lt in range(3)], axis=1)

    own = own_ref[...]
    other = other_ref[...]
    low = jnp.where(first, own, other)
    high = jnp.where(first, other, own)

    def update(weight, mom, grad, sums, stat, gain, fan):
        grad_sum, grad_proj, grad_square = sums
        mean, factor, spread, weight_sq = stat
        one = gain * factor
        two = gain * factor * factor * factor * grad_proj
        raw = one * (grad - grad_sum * (1.0 / fan)) - two * (weight - mean)
        square = (
            one * one * (grad_square - grad_sum * grad_sum * (1.0 / fan))
            - 2.0 * one * two * grad_proj
            + two * two * spread
        )
        square = jnp.maximum(square, 0.0)
        clip = jnp.minimum(1.0, clip_ratio * jnp.sqrt(weight_sq) * lax.rsqrt(square + norm_eps))
        clipped = raw * clip
        new = momentum_rate * mom + clipped
        return weight - learn_rate * (clipped + momentum_rate * new), new

    conv_sums = [line(from_both, 2 * n) for n in range(3)]
    conv_stat = [sc_ref[n : n + 1, :] for n in range(4)]
    for rows, grad in ((slice(0, 5), low[0:5, :]), (slice(5, 9), high[0:4, :])):
        weight, mom = update(
            cw_ref[rows, :], cm_ref[rows, :], grad, conv_sums, conv_stat, cg_ref[...], CONV_FAN
        )
        ncw_ref[rows, :] = weight
        ncm_ref[rows, :] = mom
    for part, (block, total) in enumerate(((low, from_low), (high, from_high))):
        lanes = slice(part * CH, (part + 1) * CH)
        weight, mom = update(
            pw_ref[:, lanes], pm_ref[:, lanes], block[5:8, :],
            [line(total, 2 * n + 1) for n in range(3)],
            [sp_ref[n : n + 1, lanes] for n in range(4)], pg_ref[:, lanes], PROJ_FAN,
        )
        npw_ref[:, lanes] = weight
        npm_ref[:, lanes] = mom


def update_call(*args):
    vmem = pl.BlockSpec(memory_space=pltpu.VMEM)
    return pl.pallas_call(
        update_kernel,
        out_shape=(
            jax.ShapeDtypeStruct((9, CH), F32),
            jax.ShapeDtypeStruct((9, CH), F32),
            jax.ShapeDtypeStruct((3, OUT), F32),
            jax.ShapeDtypeStruct((3, OUT), F32),
        ),
        in_specs=[vmem] * len(args),
        out_specs=(vmem,) * 4,
        compiler_params=small(),
        name="update",
    )(*args)


def swap(a, axis):
    return lax.ppermute(a, axis, [(0, 1), (1, 0)])


def copies(a, axis):
    n = lax.axis_size(axis)
    return lax.all_to_all(jnp.broadcast_to(a[None], (n, *a.shape)), axis, 0, 0, tiled=True)


def local(
    block_input, output_grad, conv_weight, conv_gain, conv_momentum, proj_weight, proj_gain,
    proj_momentum,
):
    cw, cm, pw, pm = conv_weight.T, conv_momentum.T, proj_weight.T, proj_momentum.T
    cg, pg = conv_gain.reshape(1, CH), proj_gain.reshape(1, OUT)
    x, og = block_input[0], output_grad[0]

    mine, edge = pack_call(cw, pw, x, og)
    halo = swap(edge, "rows")
    w_own = lax.all_to_all(mine, "z", 0, 0, tiled=True)
    w_own, halo = lax.optimization_barrier((w_own, halo))
    w_own = w_own.swapaxes(0, 1).reshape(64, CH)
    wa = copies(w_own, PLANE).reshape(1024, CH)
    wb = swap(wa, "core")
    acat = patches_call(x, halo)
    own, send, sc, sp, wcb, pp = main_call(wa, wb, acat, og, halo, cg, pg)

    pair = (own + swap(send, "core").astype(F32)).astype(BF16).reshape(16, 64, CH)
    pair, pp = lax.optimization_barrier((pair, pp))
    input_grad = input_call(x, wcb, pp)
    plane = lax.all_to_all(pair, PLANE, 0, 0, tiled=True).astype(F32).sum(axis=0).astype(BF16)
    arr = copies(plane, "z")
    msg, blk = moments_call(arr, w_own, sc, sp)
    other = swap(blk, "rows")
    stat = lax.all_to_all(msg, ("y", "x", "core", "rows"), 0, 0, tiled=True)
    ncw, ncm, npw, npm = update_call(
        stat, blk, other, cw, cm, pw, pm, sc, sp, cg, pg
    )
    return input_grad[None], ncw.T, ncm.T, npw.T, npm.T


def solution(mesh):
    split = Mesh(
        mesh.devices.reshape(8, 4, 2, 2, mesh.shape["rows"]), ("z", "y", "x", "core", "rows")
    )
    maps = P(BATCH, "rows", None, None)
    columns = P(None, BATCH)
    return jax.shard_map(
        local,
        mesh=split,
        in_specs=(maps, maps, columns, P(), columns, columns, P(), columns),
        out_specs=(maps, columns, columns, columns, columns),
        check_vma=False,
    )
```

```python
import jax
import jax.numpy as jnp
from jax import lax
from jax.experimental import pallas as pl
from jax.experimental.pallas import tpu as pltpu
from jax.sharding import Mesh
from jax.sharding import PartitionSpec as P

CH = 384
GW = 128
OUT = 768
CONV_FAN = 9 * GW
PROJ_FAN = CH
ROWS = 8
COLS = 64
BATCH = ("z", "y", "x", "core")
PLANE = ("y", "x", "rows")

ws_eps = 0.0001
clip_ratio = 0.05
momentum_rate = 0.9
learn_rate = 1.6
norm_eps = 1e-06

F32 = jnp.float32
BF16 = jnp.bfloat16


def gelu_parts(v):
    k = 0.7978845608028654
    sq = v * v
    t = jnp.tanh(k * (v + 0.044715 * (v * sq)))
    half = 0.5 * (1.0 + t)
    slope = half + 0.5 * v * (1.0 - t * t) * (k * (1.0 + 3.0 * 0.044715 * sq))
    return v * half, slope


def shifted(v, step, col):
    n = v.shape[0]
    moved = pltpu.roll(v, (-step) % n, 0)
    edge = COLS - 1 if step > 0 else 0
    return jnp.where(col == edge, 0.0, moved)


def cost(flops, nbytes):
    return pl.CostEstimate(flops=flops, bytes_accessed=nbytes, transcendentals=0)


def small(nbytes=4 * 1024 * 1024):
    return pltpu.CompilerParams(vmem_limit_bytes=nbytes)


def pack_kernel(cw_hbm, pw_hbm, x_hbm, og_hbm, out_ref, edge_ref, cw_ref, pw_ref, sems):
    h = lax.axis_index("rows")
    last = 1 - h
    moves = [
        (cw_hbm, cw_ref),
        (pw_hbm, pw_ref),
        (x_hbm.at[pl.ds(last * (ROWS - 2), 2)], edge_ref.at[pl.ds(0, 2)]),
        (og_hbm.at[last * (ROWS - 1), :, pl.ds(0, CH)], edge_ref.at[2]),
        (og_hbm.at[last * (ROWS - 1), :, pl.ds(CH, CH)], edge_ref.at[3]),
    ]
    moves = [pltpu.make_async_copy(*m, sems.at[n]) for n, m in enumerate(moves)]
    for m in moves:
        m.start()
    moves[0].wait()
    moves[1].wait()
    low = jnp.concatenate([cw_ref[0:5, :], pw_ref[:, 0:CH]], axis=0)
    high = jnp.concatenate([cw_ref[5:9, :], jnp.zeros((1, CH), F32), pw_ref[:, CH:OUT]], axis=0)
    mine = jnp.where(h == 0, low, high)
    for k in range(8):
        out_ref[k] = mine
    for m in moves[2:]:
        m.wait()


def pack_call(cw, pw, x, og):
    vmem = pl.BlockSpec(memory_space=pltpu.VMEM)
    far = pl.BlockSpec(memory_space=pltpu.HBM)
    return pl.pallas_call(
        pack_kernel,
        out_shape=(
            jax.ShapeDtypeStruct((8, 8, CH), F32),
            jax.ShapeDtypeStruct((4, COLS, CH), BF16),
        ),
        in_specs=[far] * 4,
        out_specs=(vmem, vmem),
        scratch_shapes=[
            pltpu.VMEM((9, CH), F32),
            pltpu.VMEM((3, OUT), F32),
            pltpu.SemaphoreType.DMA((5,)),
        ],
        compiler_params=small(),
        name="pack",
    )(cw, pw, x, og)


def patches_kernel(x_ref, og_ref, halo_ref, acat_ref, og9, xs):
    h = lax.axis_index("rows")
    og9[pl.ds(h, ROWS)] = og_ref[...]
    at_halo = ROWS * (1 - h)
    og9[at_halo, :, 0:CH] = halo_ref[2]
    og9[at_halo, :, CH:OUT] = halo_ref[3]
    xs[pl.ds(1 + h, ROWS)] = x_ref[...]
    zero_row = jnp.zeros((COLS, CH), BF16)

    @pl.when(h == 0)
    def _():
        xs[0] = zero_row
        xs[9] = halo_ref[0]
        xs[10] = halo_ref[1]

    @pl.when(h == 1)
    def _():
        xs[0] = halo_ref[0]
        xs[1] = halo_ref[1]
        xs[10] = zero_row

    col = lax.broadcasted_iota(jnp.int32, (11 * COLS, GW), 0) % COLS
    for g in range(3):
        lanes = slice(g * GW, (g + 1) * GW)
        act = gelu_parts(xs[:, :, lanes].reshape(11 * COLS, GW).astype(F32))[0]
        for j, piece in enumerate((shifted(act, -1, col), act, shifted(act, 1, col))):
            acat_ref[g, :, :, j * GW : (j + 1) * GW] = piece.astype(BF16).reshape(11, COLS, GW)


def patches_call(x, og, halo):
    vmem = pl.BlockSpec(memory_space=pltpu.VMEM)
    return pl.pallas_call(
        patches_kernel,
        out_shape=(
            jax.ShapeDtypeStruct((3, 11, COLS, 3 * GW), BF16),
            jax.ShapeDtypeStruct((9, COLS, OUT), BF16),
        ),
        in_specs=[vmem] * 3,
        out_specs=(vmem,) * 2,
        scratch_shapes=[pltpu.VMEM((11, COLS, CH), BF16)],
        compiler_params=pltpu.CompilerParams(vmem_limit_bytes=12 * 1024 * 1024),
        cost_estimate=cost(8 * 10**6, 2 * 10**6),
        name="patches",
    )(x, og, halo)


def strided(core, yx, kind, j):
    wide, apart = (9, 144) if kind == "c" else (3, 48)
    return pl.ds((yx * 2 + core) * wide + j, 8, stride=apart)


def deal(core, wc, wp, out_ref):
    zero_block = jnp.zeros((8, GW), F32)
    for at in range(16):
        for lt in range(3):
            found = []
            for slot in range(8):
                kind, j = ("c", slot + 5 * (at % 2)) if slot < 5 else ("p", slot - 5)
                if j == 9:
                    found.append(zero_block)
                elif kind == "c":
                    found.append(wc[lt, strided(core, at // 2, kind, j), :])
                else:
                    found.append(wp[lt + 3 * (at % 2), strided(core, at // 2, kind, j), :])
            for slot in range(0, 8, 2):
                rows = slice(at * 64 + slot * 8, at * 64 + slot * 8 + 16)
                pair = jnp.concatenate(found[slot : slot + 2], axis=0)
                out_ref[rows, lt * GW : (lt + 1) * GW] = pair.astype(out_ref.dtype)


def main_kernel(
    wa_ref, wb_ref, acat, og9, cg_ref, pg_ref,
    send_ref, sc_ref, sp_ref, wcb, pp, wc, wp,
    wpb, hid,
):
    h = lax.axis_index("rows")
    core = lax.axis_index("core")
    zero_row = jnp.zeros((COLS, CH), BF16)

    halves = (wa_ref, wb_ref)
    cores = (core, 1 - core)

    def pieces():
        for part in range(2):
            for yx in range(8):
                for s in range(5):
                    yield "c", part, yx, 2 * yx, s, s
                for s in range(4):
                    yield "c", part, yx, 2 * yx + 1, s, 5 + s
                for s in range(3):
                    yield "a", part, yx, 2 * yx, 5 + s, s
                    yield "b", part, yx, 2 * yx + 1, 5 + s, s

    def block(part, at, slot):
        return halves[part][at * 64 + slot * 8 : at * 64 + slot * 8 + 8, :]

    acc = {k: jnp.zeros((8, CH), F32) for k in "cab"}
    sq = {k: jnp.zeros((8, CH), F32) for k in "cab"}
    for kind, part, yx, at, slot, _ in pieces():
        v = block(part, at, slot)
        acc[kind] = acc[kind] + v
        sq[kind] = sq[kind] + v * v
    fan = {"c": CONV_FAN, "a": PROJ_FAN, "b": PROJ_FAN}
    mean = {k: jnp.sum(acc[k], axis=0, keepdims=True) * (1.0 / fan[k]) for k in "cab"}
    weight_sq = {k: jnp.sum(sq[k], axis=0, keepdims=True) for k in "cab"}
    spread = {k: jnp.zeros((8, CH), F32) for k in "cab"}
    for kind, part, yx, at, slot, _ in pieces():
        v = block(part, at, slot) - mean[kind]
        spread[kind] = spread[kind] + v * v
    spread = {k: jnp.sum(spread[k], axis=0, keepdims=True) for k in "cab"}
    factor = {k: lax.rsqrt(spread[k] + ws_eps) for k in "cab"}
    gain = {"c": cg_ref[...], "a": pg_ref[:, 0:CH], "b": pg_ref[:, CH:OUT]}
    scale = {k: gain[k] * factor[k] for k in "cab"}
    for n, stat in enumerate((mean, factor, spread, weight_sq)):
        sc_ref[n : n + 1, :] = stat["c"]
        sp_ref[n : n + 1, 0:CH] = stat["a"]
        sp_ref[n : n + 1, CH:OUT] = stat["b"]
    sc_ref[4:8, :] = jnp.zeros((4, CH), F32)
    sp_ref[4:8, :] = jnp.zeros((4, OUT), F32)
    for kind, part, yx, at, slot, j in pieces():
        v = scale[kind] * (block(part, at, slot) - mean[kind])
        for lt in range(3):
            piece = v[:, lt * GW : (lt + 1) * GW]
            if kind == "c":
                wc[lt, strided(cores[part], yx, kind, j), :] = piece
            else:
                wp[lt if kind == "a" else lt + 3, strided(cores[part], yx, kind, j), :] = piece
    for g in range(3):
        wcb[g] = wc[g].astype(BF16)
    for n in range(6):
        wpb[:, n * GW : (n + 1) * GW] = wp[n].astype(BF16)

    px9 = 9 * COLS
    og_all = og9[...].reshape(px9, OUT)
    for g in range(3):
        lanes = slice(g * GW, (g + 1) * GW)
        pre = jnp.zeros((px9, GW), F32)
        for i in range(3):
            pre = pre + jnp.dot(
                acat[g, i : i + 9].reshape(px9, 3 * GW),
                wcb[g, i * 3 * GW : (i + 1) * 3 * GW, :],
                preferred_element_type=F32,
            )
        value, slope = gelu_parts(pre)
        hid[:, :, lanes] = value.astype(BF16).reshape(9, COLS, GW)
        hidden_grad = lax.dot_general(
            og_all, wpb[lanes, :], (((1,), (1,)), ((), ())), preferred_element_type=F32
        )
        pre_grad = (hidden_grad * slope).astype(BF16)
        pp[pl.ds(1 - h, 9), :, lanes] = pre_grad.reshape(9, COLS, GW)
    pp[9 * h] = zero_row

    px = ROWS * COLS
    og_own = og9[pl.ds(h, ROWS)].reshape(px, OUT)
    for g in range(3):
        lanes = slice(g * GW, (g + 1) * GW)
        part = lax.dot_general(
            hid[pl.ds(h, ROWS), :, lanes].reshape(px, GW), og_own,
            (((0,), (0,)), ((), ())), preferred_element_type=F32,
        )
        for n in range(6):
            wp[n, lanes, :] = part[:, n * GW : (n + 1) * GW]
        grad_own = pp[1 : 1 + ROWS, :, lanes].reshape(px, GW)
        for i in range(3):
            wc[g, i * 3 * GW : (i + 1) * 3 * GW, :] = lax.dot_general(
                acat[g, pl.ds(h + i, ROWS)].reshape(px, 3 * GW), grad_own,
                (((0,), (0,)), ((), ())), preferred_element_type=F32,
            )
    deal(1 - core, wc, wp, send_ref)


def main_call(wa, wb, acat, og9, conv_gain, proj_gain):
    vmem = pl.BlockSpec(memory_space=pltpu.VMEM)
    return pl.pallas_call(
        main_kernel,
        out_shape=(
            jax.ShapeDtypeStruct((1024, CH), BF16),
            jax.ShapeDtypeStruct((8, CH), F32),
            jax.ShapeDtypeStruct((8, OUT), F32),
            jax.ShapeDtypeStruct((3, CONV_FAN, GW), BF16),
            jax.ShapeDtypeStruct((10, COLS, CH), BF16),
            jax.ShapeDtypeStruct((3, CONV_FAN, GW), F32),
            jax.ShapeDtypeStruct((6, PROJ_FAN, GW), F32),
        ),
        in_specs=[vmem] * 6,
        out_specs=(vmem,) * 7,
        scratch_shapes=[
            pltpu.VMEM((PROJ_FAN, OUT), BF16),
            pltpu.VMEM((9, COLS, CH), BF16),
        ],
        compiler_params=pltpu.CompilerParams(vmem_limit_bytes=32 * 1024 * 1024),
        cost_estimate=cost(15 * 10**8, 10**7),
        name="block",
    )(wa, wb, acat, og9, conv_gain, proj_gain)


def own_kernel(wc, wp, own_ref):
    deal(lax.axis_index("core"), wc, wp, own_ref)


def own_call(wc, wp):
    vmem = pl.BlockSpec(memory_space=pltpu.VMEM)
    return pl.pallas_call(
        own_kernel,
        out_shape=jax.ShapeDtypeStruct((1024, CH), F32),
        in_specs=[vmem] * 2,
        out_specs=vmem,
        compiler_params=small(8 * 1024 * 1024),
        cost_estimate=cost(10**6, 5 * 10**6),
        name="own_half",
    )(wc, wp)


def input_kernel(x_ref, wcb, pp, ig_ref, psh):
    px = ROWS * COLS
    col = lax.broadcasted_iota(jnp.int32, (10 * COLS, GW), 0) % COLS
    for g in range(3):
        lanes = slice(g * GW, (g + 1) * GW)
        grad = pp[:, :, lanes].reshape(10 * COLS, GW).astype(F32)
        psh[0] = shifted(grad, 1, col).astype(BF16)
        psh[1] = grad.astype(BF16)
        psh[2] = shifted(grad, -1, col).astype(BF16)
        total = jnp.zeros((px, GW), F32)
        for i in range(3):
            for j in range(3):
                tap = 3 * i + j
                total = total + lax.dot_general(
                    psh[j, (2 - i) * COLS : (2 - i) * COLS + px, :],
                    wcb[g, tap * GW : (tap + 1) * GW, :],
                    (((1,), (1,)), ((), ())), preferred_element_type=F32,
                )
        slope = gelu_parts(x_ref[:, :, lanes].reshape(px, GW).astype(F32))[1]
        ig_ref[:, :, lanes] = (total * slope).astype(BF16).reshape(ROWS, COLS, GW)


def input_call(x, wcb, pp):
    vmem = pl.BlockSpec(memory_space=pltpu.VMEM)
    return pl.pallas_call(
        input_kernel,
        out_shape=jax.ShapeDtypeStruct((ROWS, COLS, CH), BF16),
        in_specs=[vmem] * 3,
        out_specs=vmem,
        scratch_shapes=[pltpu.VMEM((3, 10 * COLS, GW), BF16)],
        compiler_params=pltpu.CompilerParams(vmem_limit_bytes=12 * 1024 * 1024),
        cost_estimate=cost(5 * 10**8, 3 * 10**6),
        name="input_gradient",
    )(x, wcb, pp)


def moments_kernel(arr_ref, w_ref, sc_ref, sp_ref, msg_ref, blk_ref, line_ref):
    first = lax.axis_index("rows") == 0
    z = lax.axis_index("z")
    mean_c = sc_ref[0:1, :]
    mean_p = jnp.where(first, sp_ref[0:1, 0:CH], sp_ref[0:1, CH:OUT])
    at = lax.broadcasted_iota(jnp.int32, (8, CH), 0)
    sums = []
    for slot in range(8):
        rows = slice(slot * 8, slot * 8 + 8)
        grad = arr_ref[0, rows, :].astype(F32)
        for k in range(1, 8):
            grad = grad + arr_ref[k, rows, :].astype(F32)
        grad = grad * (1.0 / 128.0)
        cent = w_ref[rows, :] - (mean_c if slot < 5 else mean_p)
        sums.append((grad, grad * cent, grad * grad))
        blk_ref[slot : slot + 1, :] = jnp.sum(
            jnp.where(at == z, grad, 0.0), axis=0, keepdims=True
        )
    lines = []
    for n in range(3):
        conv = sums[0][n] + sums[1][n] + sums[2][n] + sums[3][n] + sums[4][n]
        proj = sums[5][n] + sums[6][n] + sums[7][n]
        lines.append(jnp.sum(conv, axis=0, keepdims=True))
        lines.append(jnp.sum(proj, axis=0, keepdims=True))
    for n, line in enumerate(lines):
        for lt in range(3):
            line_ref[3 * n + lt : 3 * n + lt + 1, :] = line[:, lt * GW : (lt + 1) * GW]
    line_ref[18:24, :] = jnp.zeros((6, GW), F32)
    message = line_ref[...]
    for peer in range(32):
        msg_ref[peer] = message


def moments_call(arr, w_own, sc, sp):
    vmem = pl.BlockSpec(memory_space=pltpu.VMEM)
    return pl.pallas_call(
        moments_kernel,
        out_shape=(
            jax.ShapeDtypeStruct((32, 24, GW), F32),
            jax.ShapeDtypeStruct((8, CH), F32),
        ),
        in_specs=[vmem] * 4,
        out_specs=(vmem,) * 2,
        scratch_shapes=[pltpu.VMEM((24, GW), F32)],
        compiler_params=small(),
        name="moments",
    )(arr, w_own, sc, sp)


def update_kernel(
    stat_ref, own_ref, other_ref, cw_ref, cm_ref, pw_ref, pm_ref, sc_ref, sp_ref,
    cg_ref, pg_ref, ncw_ref, ncm_ref, npw_ref, npm_ref,
):
    first = lax.axis_index("rows") == 0
    from_low, from_high = stat_ref[0], stat_ref[1]
    for k in range(2, 32, 2):
        from_low = from_low + stat_ref[k]
        from_high = from_high + stat_ref[k + 1]
    from_both = from_low + from_high

    def line(total, n):
        return jnp.concatenate([total[3 * n + lt : 3 * n + lt + 1, :] for lt in range(3)], axis=1)

    own = own_ref[...]
    other = other_ref[...]
    low = jnp.where(first, own, other)
    high = jnp.where(first, other, own)

    def update(weight, mom, grad, sums, stat, gain, fan):
        grad_sum, grad_proj, grad_square = sums
        mean, factor, spread, weight_sq = stat
        one = gain * factor
        two = gain * factor * factor * factor * grad_proj
        raw = one * (grad - grad_sum * (1.0 / fan)) - two * (weight - mean)
        square = (
            one * one * (grad_square - grad_sum * grad_sum * (1.0 / fan))
            - 2.0 * one * two * grad_proj
            + two * two * spread
        )
        square = jnp.maximum(square, 0.0)
        clip = jnp.minimum(1.0, clip_ratio * jnp.sqrt(weight_sq) * lax.rsqrt(square + norm_eps))
        clipped = raw * clip
        new = momentum_rate * mom + clipped
        return weight - learn_rate * (clipped + momentum_rate * new), new

    conv_sums = [line(from_both, 2 * n) for n in range(3)]
    conv_stat = [sc_ref[n : n + 1, :] for n in range(4)]
    for rows, grad in ((slice(0, 5), low[0:5, :]), (slice(5, 9), high[0:4, :])):
        weight, mom = update(
            cw_ref[rows, :], cm_ref[rows, :], grad, conv_sums, conv_stat, cg_ref[...], CONV_FAN
        )
        ncw_ref[rows, :] = weight
        ncm_ref[rows, :] = mom
    for part, (block, total) in enumerate(((low, from_low), (high, from_high))):
        lanes = slice(part * CH, (part + 1) * CH)
        weight, mom = update(
            pw_ref[:, lanes], pm_ref[:, lanes], block[5:8, :],
            [line(total, 2 * n + 1) for n in range(3)],
            [sp_ref[n : n + 1, lanes] for n in range(4)], pg_ref[:, lanes], PROJ_FAN,
        )
        npw_ref[:, lanes] = weight
        npm_ref[:, lanes] = mom


def update_call(*args):
    vmem = pl.BlockSpec(memory_space=pltpu.VMEM)
    return pl.pallas_call(
        update_kernel,
        out_shape=(
            jax.ShapeDtypeStruct((9, CH), F32),
            jax.ShapeDtypeStruct((9, CH), F32),
            jax.ShapeDtypeStruct((3, OUT), F32),
            jax.ShapeDtypeStruct((3, OUT), F32),
        ),
        in_specs=[vmem] * len(args),
        out_specs=(vmem,) * 4,
        compiler_params=small(),
        name="update",
    )(*args)


def swap(a, axis):
    return lax.ppermute(a, axis, [(0, 1), (1, 0)])


def copies(a, axis):
    n = lax.axis_size(axis)
    return lax.all_to_all(jnp.broadcast_to(a[None], (n, *a.shape)), axis, 0, 0, tiled=True)


def local(
    block_input, output_grad, conv_weight, conv_gain, conv_momentum, proj_weight, proj_gain,
    proj_momentum,
):
    cw, cm, pw, pm = conv_weight.T, conv_momentum.T, proj_weight.T, proj_momentum.T
    cg, pg = conv_gain.reshape(1, CH), proj_gain.reshape(1, OUT)
    x, og = block_input[0], output_grad[0]

    mine, edge = pack_call(cw, pw, x, og)
    halo = swap(edge, "rows")
    w_own = lax.all_to_all(mine, "z", 0, 0, tiled=True)
    w_own, halo = lax.optimization_barrier((w_own, halo))
    w_own = w_own.swapaxes(0, 1).reshape(64, CH)
    wa = copies(w_own, PLANE).reshape(1024, CH)
    wb = swap(wa, "core")
    acat, og9 = patches_call(x, og, halo)
    send, sc, sp, wcb, pp, wc, wp = main_call(wa, wb, acat, og9, cg, pg)
    own = own_call(wc, wp)

    pair = (own + swap(send, "core").astype(F32)).astype(BF16).reshape(16, 64, CH)
    pair, pp = lax.optimization_barrier((pair, pp))
    input_grad = input_call(x, wcb, pp)
    plane = lax.all_to_all(pair, PLANE, 0, 0, tiled=True).astype(F32).sum(axis=0).astype(BF16)
    arr = copies(plane, "z")
    msg, blk = moments_call(arr, w_own, sc, sp)
    other = swap(blk, "rows")
    stat = lax.all_to_all(msg, ("y", "x", "core", "rows"), 0, 0, tiled=True)
    ncw, ncm, npw, npm = update_call(
        stat, blk, other, cw, cm, pw, pm, sc, sp, cg, pg
    )
    return input_grad[None], ncw.T, ncm.T, npw.T, npm.T


def solution(mesh):
    split = Mesh(
        mesh.devices.reshape(8, 4, 2, 2, mesh.shape["rows"]), ("z", "y", "x", "core", "rows")
    )
    maps = P(BATCH, "rows", None, None)
    columns = P(None, BATCH)
    return jax.shard_map(
        local,
        mesh=split,
        in_specs=(maps, maps, columns, P(), columns, columns, P(), columns),
        out_specs=(maps, columns, columns, columns, columns),
        check_vma=False,
    )
```

```python
import jax
import jax.numpy as jnp
from jax import lax
from jax.experimental import pallas as pl
from jax.experimental.pallas import tpu as pltpu
from jax.sharding import Mesh
from jax.sharding import PartitionSpec as P

CH = 384
GW = 128
OUT = 768
CONV_FAN = 9 * GW
PROJ_FAN = CH
ROWS = 8
COLS = 64
BATCH = ("z", "y", "x", "core")
PLANE = ("y", "x", "rows")

ws_eps = 0.0001
clip_ratio = 0.05
momentum_rate = 0.9
learn_rate = 1.6
norm_eps = 1e-06

F32 = jnp.float32
BF16 = jnp.bfloat16


def gelu_parts(v):
    k = 0.7978845608028654
    sq = v * v
    t = jnp.tanh(k * (v + 0.044715 * (v * sq)))
    half = 0.5 * (1.0 + t)
    slope = half + 0.5 * v * (1.0 - t * t) * (k * (1.0 + 3.0 * 0.044715 * sq))
    return v * half, slope


def shifted(v, step, col):
    n = v.shape[0]
    moved = pltpu.roll(v, (-step) % n, 0)
    edge = COLS - 1 if step > 0 else 0
    return jnp.where(col == edge, 0.0, moved)


def cost(flops, nbytes):
    return pl.CostEstimate(flops=flops, bytes_accessed=nbytes, transcendentals=0)


def small(nbytes=4 * 1024 * 1024):
    return pltpu.CompilerParams(vmem_limit_bytes=nbytes)


def pack_kernel(cw_hbm, pw_hbm, x_hbm, og_hbm, out_ref, edge_ref, cw_ref, pw_ref, sems):
    h = lax.axis_index("rows")
    last = 1 - h
    moves = [
        (cw_hbm, cw_ref),
        (pw_hbm, pw_ref),
        (x_hbm.at[pl.ds(last * (ROWS - 2), 2)], edge_ref.at[pl.ds(0, 2)]),
        (og_hbm.at[last * (ROWS - 1), :, pl.ds(0, CH)], edge_ref.at[2]),
        (og_hbm.at[last * (ROWS - 1), :, pl.ds(CH, CH)], edge_ref.at[3]),
    ]
    moves = [pltpu.make_async_copy(*m, sems.at[n]) for n, m in enumerate(moves)]
    for m in moves:
        m.start()
    moves[0].wait()
    moves[1].wait()
    low = jnp.concatenate([cw_ref[0:5, :], pw_ref[:, 0:CH]], axis=0)
    high = jnp.concatenate([cw_ref[5:9, :], jnp.zeros((1, CH), F32), pw_ref[:, CH:OUT]], axis=0)
    mine = jnp.where(h == 0, low, high)
    for k in range(8):
        out_ref[k] = mine
    for m in moves[2:]:
        m.wait()


def pack_call(cw, pw, x, og):
    vmem = pl.BlockSpec(memory_space=pltpu.VMEM)
    far = pl.BlockSpec(memory_space=pl.ANY)
    return pl.pallas_call(
        pack_kernel,
        out_shape=(
            jax.ShapeDtypeStruct((8, 8, CH), F32),
            jax.ShapeDtypeStruct((4, COLS, CH), BF16),
        ),
        in_specs=[far] * 4,
        out_specs=(vmem, vmem),
        scratch_shapes=[
            pltpu.VMEM((9, CH), F32),
            pltpu.VMEM((3, OUT), F32),
            pltpu.SemaphoreType.DMA((5,)),
        ],
        compiler_params=small(60 * 1024 * 1024),
        name="pack",
    )(cw, pw, x, og)


def patches_kernel(x_ref, og_ref, halo_ref, acat_ref, og9, xs):
    h = lax.axis_index("rows")
    og9[pl.ds(h, ROWS)] = og_ref[...]
    at_halo = ROWS * (1 - h)
    og9[at_halo, :, 0:CH] = halo_ref[2]
    og9[at_halo, :, CH:OUT] = halo_ref[3]
    xs[pl.ds(1 + h, ROWS)] = x_ref[...]
    zero_row = jnp.zeros((COLS, CH), BF16)

    @pl.when(h == 0)
    def _():
        xs[0] = zero_row
        xs[9] = halo_ref[0]
        xs[10] = halo_ref[1]

    @pl.when(h == 1)
    def _():
        xs[0] = halo_ref[0]
        xs[1] = halo_ref[1]
        xs[10] = zero_row

    col = lax.broadcasted_iota(jnp.int32, (11 * COLS, GW), 0) % COLS
    for g in range(3):
        lanes = slice(g * GW, (g + 1) * GW)
        act = gelu_parts(xs[:, :, lanes].reshape(11 * COLS, GW).astype(F32))[0]
        for j, piece in enumerate((shifted(act, -1, col), act, shifted(act, 1, col))):
            acat_ref[g, :, :, j * GW : (j + 1) * GW] = piece.astype(BF16).reshape(11, COLS, GW)


def patches_call(x, og, halo):
    vmem = pl.BlockSpec(memory_space=pltpu.VMEM)
    return pl.pallas_call(
        patches_kernel,
        out_shape=(
            jax.ShapeDtypeStruct((3, 11, COLS, 3 * GW), BF16),
            jax.ShapeDtypeStruct((9, COLS, OUT), BF16),
        ),
        in_specs=[vmem] * 3,
        out_specs=(vmem,) * 2,
        scratch_shapes=[pltpu.VMEM((11, COLS, CH), BF16)],
        compiler_params=pltpu.CompilerParams(vmem_limit_bytes=12 * 1024 * 1024),
        cost_estimate=cost(8 * 10**6, 2 * 10**6),
        name="patches",
    )(x, og, halo)


def strided(core, yx, kind, j):
    wide, apart = (9, 144) if kind == "c" else (3, 48)
    return pl.ds((yx * 2 + core) * wide + j, 8, stride=apart)


def deal(core, wc, wp, out_ref):
    zero_block = jnp.zeros((8, GW), F32)
    for at in range(16):
        for lt in range(3):
            found = []
            for slot in range(8):
                kind, j = ("c", slot + 5 * (at % 2)) if slot < 5 else ("p", slot - 5)
                if j == 9:
                    found.append(zero_block)
                elif kind == "c":
                    found.append(wc[lt, strided(core, at // 2, kind, j), :])
                else:
                    found.append(wp[lt + 3 * (at % 2), strided(core, at // 2, kind, j), :])
            for slot in range(0, 8, 2):
                rows = slice(at * 64 + slot * 8, at * 64 + slot * 8 + 16)
                pair = jnp.concatenate(found[slot : slot + 2], axis=0)
                out_ref[rows, lt * GW : (lt + 1) * GW] = pair.astype(out_ref.dtype)


def main_kernel(
    wa_ref, wb_ref, acat, og9, cg_ref, pg_ref,
    send_ref, sc_ref, sp_ref, wcb, pp, wc, wp,
    wpb, hid,
):
    h = lax.axis_index("rows")
    core = lax.axis_index("core")
    zero_row = jnp.zeros((COLS, CH), BF16)

    halves = (wa_ref, wb_ref)
    cores = (core, 1 - core)

    def pieces():
        for part in range(2):
            for yx in range(8):
                for s in range(5):
                    yield "c", part, yx, 2 * yx, s, s
                for s in range(4):
                    yield "c", part, yx, 2 * yx + 1, s, 5 + s
                for s in range(3):
                    yield "a", part, yx, 2 * yx, 5 + s, s
                    yield "b", part, yx, 2 * yx + 1, 5 + s, s

    def block(part, at, slot):
        return halves[part][at * 64 + slot * 8 : at * 64 + slot * 8 + 8, :]

    acc = {k: jnp.zeros((8, CH), F32) for k in "cab"}
    sq = {k: jnp.zeros((8, CH), F32) for k in "cab"}
    for kind, part, yx, at, slot, _ in pieces():
        v = block(part, at, slot)
        acc[kind] = acc[kind] + v
        sq[kind] = sq[kind] + v * v
    fan = {"c": CONV_FAN, "a": PROJ_FAN, "b": PROJ_FAN}
    mean = {k: jnp.sum(acc[k], axis=0, keepdims=True) * (1.0 / fan[k]) for k in "cab"}
    weight_sq = {k: jnp.sum(sq[k], axis=0, keepdims=True) for k in "cab"}
    spread = {k: jnp.zeros((8, CH), F32) for k in "cab"}
    for kind, part, yx, at, slot, _ in pieces():
        v = block(part, at, slot) - mean[kind]
        spread[kind] = spread[kind] + v * v
    spread = {k: jnp.sum(spread[k], axis=0, keepdims=True) for k in "cab"}
    factor = {k: lax.rsqrt(spread[k] + ws_eps) for k in "cab"}
    gain = {"c": cg_ref[...], "a": pg_ref[:, 0:CH], "b": pg_ref[:, CH:OUT]}
    scale = {k: gain[k] * factor[k] for k in "cab"}
    for n, stat in enumerate((mean, factor, spread, weight_sq)):
        sc_ref[n : n + 1, :] = stat["c"]
        sp_ref[n : n + 1, 0:CH] = stat["a"]
        sp_ref[n : n + 1, CH:OUT] = stat["b"]
    sc_ref[4:8, :] = jnp.zeros((4, CH), F32)
    sp_ref[4:8, :] = jnp.zeros((4, OUT), F32)
    for kind, part, yx, at, slot, j in pieces():
        v = scale[kind] * (block(part, at, slot) - mean[kind])
        for lt in range(3):
            piece = v[:, lt * GW : (lt + 1) * GW]
            if kind == "c":
                wc[lt, strided(cores[part], yx, kind, j), :] = piece
            else:
                wp[lt if kind == "a" else lt + 3, strided(cores[part], yx, kind, j), :] = piece
    for g in range(3):
        wcb[g] = wc[g].astype(BF16)
    for n in range(6):
        wpb[:, n * GW : (n + 1) * GW] = wp[n].astype(BF16)

    px9 = 9 * COLS
    og_all = og9[...].reshape(px9, OUT)
    for g in range(3):
        lanes = slice(g * GW, (g + 1) * GW)
        pre = jnp.zeros((px9, GW), F32)
        for i in range(3):
            pre = pre + jnp.dot(
                acat[g, i : i + 9].reshape(px9, 3 * GW),
                wcb[g, i * 3 * GW : (i + 1) * 3 * GW, :],
                preferred_element_type=F32,
            )
        value, slope = gelu_parts(pre)
        hid[:, :, lanes] = value.astype(BF16).reshape(9, COLS, GW)
        hidden_grad = lax.dot_general(
            og_all, wpb[lanes, :], (((1,), (1,)), ((), ())), preferred_element_type=F32
        )
        pre_grad = (hidden_grad * slope).astype(BF16)
        pp[pl.ds(1 - h, 9), :, lanes] = pre_grad.reshape(9, COLS, GW)
    pp[9 * h] = zero_row

    px = ROWS * COLS
    og_own = og9[pl.ds(h, ROWS)].reshape(px, OUT)
    for g in range(3):
        lanes = slice(g * GW, (g + 1) * GW)
        part = lax.dot_general(
            hid[pl.ds(h, ROWS), :, lanes].reshape(px, GW), og_own,
            (((0,), (0,)), ((), ())), preferred_element_type=F32,
        )
        for n in range(6):
            wp[n, lanes, :] = part[:, n * GW : (n + 1) * GW]
        grad_own = pp[1 : 1 + ROWS, :, lanes].reshape(px, GW)
        for i in range(3):
            wc[g, i * 3 * GW : (i + 1) * 3 * GW, :] = lax.dot_general(
                acat[g, pl.ds(h + i, ROWS)].reshape(px, 3 * GW), grad_own,
                (((0,), (0,)), ((), ())), preferred_element_type=F32,
            )
    deal(1 - core, wc, wp, send_ref)


def main_call(wa, wb, acat, og9, conv_gain, proj_gain):
    vmem = pl.BlockSpec(memory_space=pltpu.VMEM)
    return pl.pallas_call(
        main_kernel,
        out_shape=(
            jax.ShapeDtypeStruct((1024, CH), BF16),
            jax.ShapeDtypeStruct((8, CH), F32),
            jax.ShapeDtypeStruct((8, OUT), F32),
            jax.ShapeDtypeStruct((3, CONV_FAN, GW), BF16),
            jax.ShapeDtypeStruct((10, COLS, CH), BF16),
            jax.ShapeDtypeStruct((3, CONV_FAN, GW), F32),
            jax.ShapeDtypeStruct((6, PROJ_FAN, GW), F32),
        ),
        in_specs=[vmem] * 6,
        out_specs=(vmem,) * 7,
        scratch_shapes=[
            pltpu.VMEM((PROJ_FAN, OUT), BF16),
            pltpu.VMEM((9, COLS, CH), BF16),
        ],
        compiler_params=pltpu.CompilerParams(vmem_limit_bytes=32 * 1024 * 1024),
        cost_estimate=cost(15 * 10**8, 10**7),
        name="block",
    )(wa, wb, acat, og9, conv_gain, proj_gain)


def own_kernel(wc, wp, own_ref):
    deal(lax.axis_index("core"), wc, wp, own_ref)


def own_call(wc, wp):
    vmem = pl.BlockSpec(memory_space=pltpu.VMEM)
    return pl.pallas_call(
        own_kernel,
        out_shape=jax.ShapeDtypeStruct((1024, CH), F32),
        in_specs=[vmem] * 2,
        out_specs=vmem,
        compiler_params=small(8 * 1024 * 1024),
        cost_estimate=cost(10**6, 5 * 10**6),
        name="own_half",
    )(wc, wp)


def input_kernel(x_ref, wcb, pp, ig_ref, psh):
    px = ROWS * COLS
    col = lax.broadcasted_iota(jnp.int32, (10 * COLS, GW), 0) % COLS
    for g in range(3):
        lanes = slice(g * GW, (g + 1) * GW)
        grad = pp[:, :, lanes].reshape(10 * COLS, GW).astype(F32)
        psh[0] = shifted(grad, 1, col).astype(BF16)
        psh[1] = grad.astype(BF16)
        psh[2] = shifted(grad, -1, col).astype(BF16)
        total = jnp.zeros((px, GW), F32)
        for i in range(3):
            for j in range(3):
                tap = 3 * i + j
                total = total + lax.dot_general(
                    psh[j, (2 - i) * COLS : (2 - i) * COLS + px, :],
                    wcb[g, tap * GW : (tap + 1) * GW, :],
                    (((1,), (1,)), ((), ())), preferred_element_type=F32,
                )
        slope = gelu_parts(x_ref[:, :, lanes].reshape(px, GW).astype(F32))[1]
        ig_ref[:, :, lanes] = (total * slope).astype(BF16).reshape(ROWS, COLS, GW)


def input_call(x, wcb, pp):
    vmem = pl.BlockSpec(memory_space=pltpu.VMEM)
    return pl.pallas_call(
        input_kernel,
        out_shape=jax.ShapeDtypeStruct((ROWS, COLS, CH), BF16),
        in_specs=[vmem] * 3,
        out_specs=vmem,
        scratch_shapes=[pltpu.VMEM((3, 10 * COLS, GW), BF16)],
        compiler_params=pltpu.CompilerParams(vmem_limit_bytes=12 * 1024 * 1024),
        cost_estimate=cost(5 * 10**8, 3 * 10**6),
        name="input_gradient",
    )(x, wcb, pp)


def moments_kernel(arr_ref, w_ref, sc_ref, sp_ref, msg_ref, blk_ref, line_ref):
    first = lax.axis_index("rows") == 0
    z = lax.axis_index("z")
    mean_c = sc_ref[0:1, :]
    mean_p = jnp.where(first, sp_ref[0:1, 0:CH], sp_ref[0:1, CH:OUT])
    at = lax.broadcasted_iota(jnp.int32, (8, CH), 0)
    sums = []
    for slot in range(8):
        rows = slice(slot * 8, slot * 8 + 8)
        grad = arr_ref[0, rows, :].astype(F32)
        for k in range(1, 8):
            grad = grad + arr_ref[k, rows, :].astype(F32)
        grad = grad * (1.0 / 128.0)
        cent = w_ref[rows, :] - (mean_c if slot < 5 else mean_p)
        sums.append((grad, grad * cent, grad * grad))
        blk_ref[slot : slot + 1, :] = jnp.sum(
            jnp.where(at == z, grad, 0.0), axis=0, keepdims=True
        )
    for n in range(3):
        lanes = slice(n * CH, (n + 1) * CH)
        conv = sums[0][n] + sums[1][n] + sums[2][n] + sums[3][n] + sums[4][n]
        proj = sums[5][n] + sums[6][n] + sums[7][n]
        line_ref[0:1, lanes] = jnp.sum(conv, axis=0, keepdims=True)
        line_ref[1:2, lanes] = jnp.sum(proj, axis=0, keepdims=True)
    message = line_ref[...]
    for peer in range(32):
        msg_ref[peer] = message


def moments_call(arr, w_own, sc, sp):
    vmem = pl.BlockSpec(memory_space=pltpu.VMEM)
    return pl.pallas_call(
        moments_kernel,
        out_shape=(
            jax.ShapeDtypeStruct((32, 2, 3 * CH), F32),
            jax.ShapeDtypeStruct((8, CH), F32),
        ),
        in_specs=[vmem] * 4,
        out_specs=(vmem,) * 2,
        scratch_shapes=[pltpu.VMEM((2, 3 * CH), F32)],
        compiler_params=small(),
        name="moments",
    )(arr, w_own, sc, sp)


def update_kernel(
    stat_ref, own_ref, other_ref, cw_ref, cm_ref, pw_ref, pm_ref, sc_ref, sp_ref,
    cg_ref, pg_ref, ncw_ref, ncm_ref, npw_ref, npm_ref,
):
    first = lax.axis_index("rows") == 0
    from_low, from_high = stat_ref[0], stat_ref[1]
    for k in range(2, 32, 2):
        from_low = from_low + stat_ref[k]
        from_high = from_high + stat_ref[k + 1]
    from_both = from_low + from_high

    def line(total, row, n):
        return total[row : row + 1, n * CH : (n + 1) * CH]

    own = own_ref[...]
    other = other_ref[...]
    low = jnp.where(first, own, other)
    high = jnp.where(first, other, own)

    def update(weight, mom, grad, sums, stat, gain, fan):
        grad_sum, grad_proj, grad_square = sums
        mean, factor, spread, weight_sq = stat
        one = gain * factor
        two = gain * factor * factor * factor * grad_proj
        raw = one * (grad - grad_sum * (1.0 / fan)) - two * (weight - mean)
        square = (
            one * one * (grad_square - grad_sum * grad_sum * (1.0 / fan))
            - 2.0 * one * two * grad_proj
            + two * two * spread
        )
        square = jnp.maximum(square, 0.0)
        clip = jnp.minimum(1.0, clip_ratio * jnp.sqrt(weight_sq) * lax.rsqrt(square + norm_eps))
        clipped = raw * clip
        new = momentum_rate * mom + clipped
        return weight - learn_rate * (clipped + momentum_rate * new), new

    conv_sums = [line(from_both, 0, n) for n in range(3)]
    conv_stat = [sc_ref[n : n + 1, :] for n in range(4)]
    for rows, grad in ((slice(0, 5), low[0:5, :]), (slice(5, 9), high[0:4, :])):
        weight, mom = update(
            cw_ref[rows, :], cm_ref[rows, :], grad, conv_sums, conv_stat, cg_ref[...], CONV_FAN
        )
        ncw_ref[rows, :] = weight
        ncm_ref[rows, :] = mom
    for part, (block, total) in enumerate(((low, from_low), (high, from_high))):
        lanes = slice(part * CH, (part + 1) * CH)
        weight, mom = update(
            pw_ref[:, lanes], pm_ref[:, lanes], block[5:8, :],
            [line(total, 1, n) for n in range(3)],
            [sp_ref[n : n + 1, lanes] for n in range(4)], pg_ref[:, lanes], PROJ_FAN,
        )
        npw_ref[:, lanes] = weight
        npm_ref[:, lanes] = mom


def update_call(*args):
    vmem = pl.BlockSpec(memory_space=pltpu.VMEM)
    return pl.pallas_call(
        update_kernel,
        out_shape=(
            jax.ShapeDtypeStruct((9, CH), F32),
            jax.ShapeDtypeStruct((9, CH), F32),
            jax.ShapeDtypeStruct((3, OUT), F32),
            jax.ShapeDtypeStruct((3, OUT), F32),
        ),
        in_specs=[vmem] * len(args),
        out_specs=(vmem,) * 4,
        compiler_params=small(),
        name="update",
    )(*args)


def swap(a, axis):
    return lax.ppermute(a, axis, [(0, 1), (1, 0)])


def copies(a, axis):
    n = lax.axis_size(axis)
    return lax.all_to_all(jnp.broadcast_to(a[None], (n, *a.shape)), axis, 0, 0, tiled=True)


def local(
    block_input, output_grad, conv_weight, conv_gain, conv_momentum, proj_weight, proj_gain,
    proj_momentum,
):
    cw, cm, pw, pm = conv_weight.T, conv_momentum.T, proj_weight.T, proj_momentum.T
    cg, pg = conv_gain.reshape(1, CH), proj_gain.reshape(1, OUT)
    x, og = block_input[0], output_grad[0]

    mine, edge = pack_call(cw, pw, x, og)
    halo = swap(edge, "rows")
    w_own = lax.all_to_all(mine, "z", 0, 0, tiled=True)
    w_own, halo = lax.optimization_barrier((w_own, halo))
    w_own = w_own.swapaxes(0, 1).reshape(64, CH)
    wa = copies(w_own, PLANE).reshape(1024, CH)
    wb = swap(wa, "core")
    acat, og9 = patches_call(x, og, halo)
    send, sc, sp, wcb, pp, wc, wp = main_call(wa, wb, acat, og9, cg, pg)
    own = own_call(wc, wp)

    pair = (own + swap(send, "core").astype(F32)).astype(BF16).reshape(16, 64, CH)
    pair, pp = lax.optimization_barrier((pair, pp))
    input_grad = input_call(x, wcb, pp)
    plane = lax.all_to_all(pair, PLANE, 0, 0, tiled=True).astype(F32).sum(axis=0).astype(BF16)
    arr = copies(plane, "z")
    msg, blk = moments_call(arr, w_own, sc, sp)
    other = swap(blk, "rows")
    stat = lax.all_to_all(msg, ("y", "x", "core", "rows"), 0, 0, tiled=True)
    ncw, ncm, npw, npm = update_call(
        stat, blk, other, cw, cm, pw, pm, sc, sp, cg, pg
    )
    return input_grad[None], ncw.T, ncm.T, npw.T, npm.T


def solution(mesh):
    split = Mesh(
        mesh.devices.reshape(8, 4, 2, 2, mesh.shape["rows"]), ("z", "y", "x", "core", "rows")
    )
    maps = P(BATCH, "rows", None, None)
    columns = P(None, BATCH)
    return jax.shard_map(
        local,
        mesh=split,
        in_specs=(maps, maps, columns, P(), columns, columns, P(), columns),
        out_specs=(maps, columns, columns, columns, columns),
        check_vma=False,
    )
```

```python
import jax
import jax.numpy as jnp
from jax import lax
from jax.experimental import pallas as pl
from jax.experimental.pallas import tpu as pltpu
from jax.sharding import Mesh
from jax.sharding import PartitionSpec as P

CH = 384
GW = 128
OUT = 768
CONV_FAN = 9 * GW
PROJ_FAN = CH
ROWS = 8
COLS = 64
BATCH = ("z", "y", "x", "core")
PLANE = ("rows", "x", "y")

ws_eps = 0.0001
clip_ratio = 0.05
momentum_rate = 0.9
learn_rate = 1.6
norm_eps = 1e-06

F32 = jnp.float32
BF16 = jnp.bfloat16


def gelu_parts(v):
    k = 0.7978845608028654
    sq = v * v
    t = jnp.tanh(k * (v + 0.044715 * (v * sq)))
    half = 0.5 * (1.0 + t)
    slope = half + 0.5 * v * (1.0 - t * t) * (k * (1.0 + 3.0 * 0.044715 * sq))
    return v * half, slope


def shifted(v, step, col):
    n = v.shape[0]
    moved = pltpu.roll(v, (-step) % n, 0)
    edge = COLS - 1 if step > 0 else 0
    return jnp.where(col == edge, 0.0, moved)


def cost(flops, nbytes):
    return pl.CostEstimate(flops=flops, bytes_accessed=nbytes, transcendentals=0)


def small(nbytes=4 * 1024 * 1024):
    return pltpu.CompilerParams(vmem_limit_bytes=nbytes)


def pack_kernel(cw_hbm, pw_hbm, x_hbm, og_hbm, out_ref, edge_ref, cw_ref, pw_ref, sems):
    h = lax.axis_index("rows")
    last = 1 - h
    moves = [
        (cw_hbm, cw_ref),
        (pw_hbm, pw_ref),
        (x_hbm.at[pl.ds(last * (ROWS - 2), 2)], edge_ref.at[pl.ds(0, 2)]),
        (og_hbm.at[last * (ROWS - 1), :, pl.ds(0, CH)], edge_ref.at[2]),
        (og_hbm.at[last * (ROWS - 1), :, pl.ds(CH, CH)], edge_ref.at[3]),
    ]
    moves = [pltpu.make_async_copy(*m, sems.at[n]) for n, m in enumerate(moves)]
    for m in moves:
        m.start()
    moves[0].wait()
    moves[1].wait()
    low = jnp.concatenate([cw_ref[0:5, :], pw_ref[:, 0:CH]], axis=0)
    high = jnp.concatenate([cw_ref[5:9, :], jnp.zeros((1, CH), F32), pw_ref[:, CH:OUT]], axis=0)
    mine = jnp.where(h == 0, low, high)
    for k in range(8):
        out_ref[k] = mine
    for m in moves[2:]:
        m.wait()


def pack_call(cw, pw, x, og):
    vmem = pl.BlockSpec(memory_space=pltpu.VMEM)
    far = pl.BlockSpec(memory_space=pl.ANY)
    return pl.pallas_call(
        pack_kernel,
        out_shape=(
            jax.ShapeDtypeStruct((8, 8, CH), F32),
            jax.ShapeDtypeStruct((4, COLS, CH), BF16),
        ),
        in_specs=[far] * 4,
        out_specs=(vmem, vmem),
        scratch_shapes=[
            pltpu.VMEM((9, CH), F32),
            pltpu.VMEM((3, OUT), F32),
            pltpu.SemaphoreType.DMA((5,)),
        ],
        compiler_params=small(60 * 1024 * 1024),
        name="pack",
    )(cw, pw, x, og)


def patches_kernel(x_ref, og_ref, halo_ref, acat_ref, og9, xs):
    h = lax.axis_index("rows")
    og9[pl.ds(h, ROWS)] = og_ref[...]
    at_halo = ROWS * (1 - h)
    og9[at_halo, :, 0:CH] = halo_ref[2]
    og9[at_halo, :, CH:OUT] = halo_ref[3]
    xs[pl.ds(1 + h, ROWS)] = x_ref[...]
    zero_row = jnp.zeros((COLS, CH), BF16)

    @pl.when(h == 0)
    def _():
        xs[0] = zero_row
        xs[9] = halo_ref[0]
        xs[10] = halo_ref[1]

    @pl.when(h == 1)
    def _():
        xs[0] = halo_ref[0]
        xs[1] = halo_ref[1]
        xs[10] = zero_row

    col = lax.broadcasted_iota(jnp.int32, (11 * COLS, GW), 0) % COLS
    for g in range(3):
        lanes = slice(g * GW, (g + 1) * GW)
        act = gelu_parts(xs[:, :, lanes].reshape(11 * COLS, GW).astype(F32))[0]
        for j, piece in enumerate((shifted(act, -1, col), act, shifted(act, 1, col))):
            acat_ref[g, :, :, j * GW : (j + 1) * GW] = piece.astype(BF16).reshape(11, COLS, GW)


def patches_call(x, og, halo):
    vmem = pl.BlockSpec(memory_space=pltpu.VMEM)
    return pl.pallas_call(
        patches_kernel,
        out_shape=(
            jax.ShapeDtypeStruct((3, 11, COLS, 3 * GW), BF16),
            jax.ShapeDtypeStruct((9, COLS, OUT), BF16),
        ),
        in_specs=[vmem] * 3,
        out_specs=(vmem,) * 2,
        scratch_shapes=[pltpu.VMEM((11, COLS, CH), BF16)],
        compiler_params=pltpu.CompilerParams(vmem_limit_bytes=12 * 1024 * 1024),
        cost_estimate=cost(8 * 10**6, 2 * 10**6),
        name="patches",
    )(x, og, halo)


def place(h, yx):
    return h * 8 + yx % 2 * 4 + yx // 2


def strided(core, yx, kind, j):
    wide, apart = (9, 144) if kind == "c" else (3, 48)
    return pl.ds((yx * 2 + core) * wide + j, 8, stride=apart)


def deal(core, wc, wp, out_ref):
    zero_block = jnp.zeros((8, GW), F32)
    for h, yx in [(h, yx) for h in range(2) for yx in range(8)]:
        at = place(h, yx)
        for lt in range(3):
            found = []
            for slot in range(8):
                kind, j = ("c", slot + 5 * h) if slot < 5 else ("p", slot - 5)
                if j == 9:
                    found.append(zero_block)
                elif kind == "c":
                    found.append(wc[lt, strided(core, yx, kind, j), :])
                else:
                    found.append(wp[lt + 3 * h, strided(core, yx, kind, j), :])
            for slot in range(0, 8, 2):
                rows = slice(at * 64 + slot * 8, at * 64 + slot * 8 + 16)
                pair = jnp.concatenate(found[slot : slot + 2], axis=0)
                out_ref[rows, lt * GW : (lt + 1) * GW] = pair.astype(out_ref.dtype)


def main_kernel(
    wa_ref, wb_ref, acat, og9, cg_ref, pg_ref,
    send_ref, sc_ref, sp_ref, wcb, pp, wc, wp,
    wpb, hid,
):
    h = lax.axis_index("rows")
    core = lax.axis_index("core")
    zero_row = jnp.zeros((COLS, CH), BF16)

    halves = (wa_ref, wb_ref)
    cores = (core, 1 - core)

    def pieces():
        for part in range(2):
            for yx in range(8):
                for s in range(5):
                    yield "c", part, yx, place(0, yx), s, s
                for s in range(4):
                    yield "c", part, yx, place(1, yx), s, 5 + s
                for s in range(3):
                    yield "a", part, yx, place(0, yx), 5 + s, s
                    yield "b", part, yx, place(1, yx), 5 + s, s

    def block(part, at, slot):
        return halves[part][at * 64 + slot * 8 : at * 64 + slot * 8 + 8, :]

    acc = {k: jnp.zeros((8, CH), F32) for k in "cab"}
    sq = {k: jnp.zeros((8, CH), F32) for k in "cab"}
    for kind, part, yx, at, slot, _ in pieces():
        v = block(part, at, slot)
        acc[kind] = acc[kind] + v
        sq[kind] = sq[kind] + v * v
    fan = {"c": CONV_FAN, "a": PROJ_FAN, "b": PROJ_FAN}
    mean = {k: jnp.sum(acc[k], axis=0, keepdims=True) * (1.0 / fan[k]) for k in "cab"}
    weight_sq = {k: jnp.sum(sq[k], axis=0, keepdims=True) for k in "cab"}
    spread = {k: jnp.zeros((8, CH), F32) for k in "cab"}
    for kind, part, yx, at, slot, _ in pieces():
        v = block(part, at, slot) - mean[kind]
        spread[kind] = spread[kind] + v * v
    spread = {k: jnp.sum(spread[k], axis=0, keepdims=True) for k in "cab"}
    factor = {k: lax.rsqrt(spread[k] + ws_eps) for k in "cab"}
    gain = {"c": cg_ref[...], "a": pg_ref[:, 0:CH], "b": pg_ref[:, CH:OUT]}
    scale = {k: gain[k] * factor[k] for k in "cab"}
    for n, stat in enumerate((mean, factor, spread, weight_sq)):
        sc_ref[n : n + 1, :] = stat["c"]
        sp_ref[n : n + 1, 0:CH] = stat["a"]
        sp_ref[n : n + 1, CH:OUT] = stat["b"]
    sc_ref[4:8, :] = jnp.zeros((4, CH), F32)
    sp_ref[4:8, :] = jnp.zeros((4, OUT), F32)
    for kind, part, yx, at, slot, j in pieces():
        v = scale[kind] * (block(part, at, slot) - mean[kind])
        for lt in range(3):
            piece = v[:, lt * GW : (lt + 1) * GW]
            if kind == "c":
                wc[lt, strided(cores[part], yx, kind, j), :] = piece
            else:
                wp[lt if kind == "a" else lt + 3, strided(cores[part], yx, kind, j), :] = piece
    for g in range(3):
        wcb[g] = wc[g].astype(BF16)
    for n in range(6):
        wpb[:, n * GW : (n + 1) * GW] = wp[n].astype(BF16)

    px9 = 9 * COLS
    hidden_grad = lax.dot_general(
        og9[...].reshape(px9, OUT), wpb[...], (((1,), (1,)), ((), ())), preferred_element_type=F32
    )
    for g in range(3):
        lanes = slice(g * GW, (g + 1) * GW)
        pre = jnp.zeros((px9, GW), F32)
        for i in range(3):
            pre = pre + jnp.dot(
                acat[g, i : i + 9].reshape(px9, 3 * GW),
                wcb[g, i * 3 * GW : (i + 1) * 3 * GW, :],
                preferred_element_type=F32,
            )
        value, slope = gelu_parts(pre)
        hid[:, :, lanes] = value.astype(BF16).reshape(9, COLS, GW)
        pre_grad = (hidden_grad[:, lanes] * slope).astype(BF16)
        pp[pl.ds(1 - h, 9), :, lanes] = pre_grad.reshape(9, COLS, GW)
    pp[9 * h] = zero_row

    px = ROWS * COLS
    og_own = og9[pl.ds(h, ROWS)].reshape(px, OUT)
    for g in range(3):
        lanes = slice(g * GW, (g + 1) * GW)
        part = lax.dot_general(
            hid[pl.ds(h, ROWS), :, lanes].reshape(px, GW), og_own,
            (((0,), (0,)), ((), ())), preferred_element_type=F32,
        )
        for n in range(6):
            wp[n, lanes, :] = part[:, n * GW : (n + 1) * GW]
        grad_own = pp[1 : 1 + ROWS, :, lanes].reshape(px, GW)
        for i in range(3):
            wc[g, i * 3 * GW : (i + 1) * 3 * GW, :] = lax.dot_general(
                acat[g, pl.ds(h + i, ROWS)].reshape(px, 3 * GW), grad_own,
                (((0,), (0,)), ((), ())), preferred_element_type=F32,
            )
    deal(1 - core, wc, wp, send_ref)


def main_call(wa, wb, acat, og9, conv_gain, proj_gain):
    vmem = pl.BlockSpec(memory_space=pltpu.VMEM)
    return pl.pallas_call(
        main_kernel,
        out_shape=(
            jax.ShapeDtypeStruct((1024, CH), BF16),
            jax.ShapeDtypeStruct((8, CH), F32),
            jax.ShapeDtypeStruct((8, OUT), F32),
            jax.ShapeDtypeStruct((3, CONV_FAN, GW), BF16),
            jax.ShapeDtypeStruct((10, COLS, CH), BF16),
            jax.ShapeDtypeStruct((3, CONV_FAN, GW), F32),
            jax.ShapeDtypeStruct((6, PROJ_FAN, GW), F32),
        ),
        in_specs=[vmem] * 6,
        out_specs=(vmem,) * 7,
        scratch_shapes=[
            pltpu.VMEM((PROJ_FAN, OUT), BF16),
            pltpu.VMEM((9, COLS, CH), BF16),
        ],
        compiler_params=pltpu.CompilerParams(vmem_limit_bytes=32 * 1024 * 1024),
        cost_estimate=cost(15 * 10**8, 10**7),
        name="block",
    )(wa, wb, acat, og9, conv_gain, proj_gain)


def own_kernel(wc, wp, own_ref):
    deal(lax.axis_index("core"), wc, wp, own_ref)


def own_call(wc, wp):
    vmem = pl.BlockSpec(memory_space=pltpu.VMEM)
    return pl.pallas_call(
        own_kernel,
        out_shape=jax.ShapeDtypeStruct((1024, CH), F32),
        in_specs=[vmem] * 2,
        out_specs=vmem,
        compiler_params=small(8 * 1024 * 1024),
        cost_estimate=cost(10**6, 5 * 10**6),
        name="own_half",
    )(wc, wp)


def input_kernel(x_ref, wcb, pp, ig_ref, psh):
    px = ROWS * COLS
    col = lax.broadcasted_iota(jnp.int32, (10 * COLS, GW), 0) % COLS
    for g in range(3):
        lanes = slice(g * GW, (g + 1) * GW)
        grad = pp[:, :, lanes].reshape(10 * COLS, GW).astype(F32)
        psh[0] = shifted(grad, 1, col).astype(BF16)
        psh[1] = grad.astype(BF16)
        psh[2] = shifted(grad, -1, col).astype(BF16)
        total = jnp.zeros((px, GW), F32)
        for i in range(3):
            for j in range(3):
                tap = 3 * i + j
                total = total + lax.dot_general(
                    psh[j, (2 - i) * COLS : (2 - i) * COLS + px, :],
                    wcb[g, tap * GW : (tap + 1) * GW, :],
                    (((1,), (1,)), ((), ())), preferred_element_type=F32,
                )
        slope = gelu_parts(x_ref[:, :, lanes].reshape(px, GW).astype(F32))[1]
        ig_ref[:, :, lanes] = (total * slope).astype(BF16).reshape(ROWS, COLS, GW)


def input_call(x, wcb, pp):
    vmem = pl.BlockSpec(memory_space=pltpu.VMEM)
    return pl.pallas_call(
        input_kernel,
        out_shape=jax.ShapeDtypeStruct((ROWS, COLS, CH), BF16),
        in_specs=[vmem] * 3,
        out_specs=vmem,
        scratch_shapes=[pltpu.VMEM((3, 10 * COLS, GW), BF16)],
        compiler_params=pltpu.CompilerParams(vmem_limit_bytes=12 * 1024 * 1024),
        cost_estimate=cost(5 * 10**8, 3 * 10**6),
        name="input_gradient",
    )(x, wcb, pp)


def moments_kernel(arr_ref, w_ref, sc_ref, sp_ref, msg_ref, blk_ref, line_ref):
    first = lax.axis_index("rows") == 0
    z = lax.axis_index("z")
    mean_c = sc_ref[0:1, :]
    mean_p = jnp.where(first, sp_ref[0:1, 0:CH], sp_ref[0:1, CH:OUT])
    at = lax.broadcasted_iota(jnp.int32, (8, CH), 0)
    sums = []
    for slot in range(8):
        rows = slice(slot * 8, slot * 8 + 8)
        grad = arr_ref[0, rows, :].astype(F32)
        for k in range(1, 8):
            grad = grad + arr_ref[k, rows, :].astype(F32)
        grad = grad * (1.0 / 128.0)
        cent = w_ref[rows, :] - (mean_c if slot < 5 else mean_p)
        sums.append((grad, grad * cent, grad * grad))
        blk_ref[slot : slot + 1, :] = jnp.sum(
            jnp.where(at == z, grad, 0.0), axis=0, keepdims=True
        )
    for n in range(3):
        lanes = slice(n * CH, (n + 1) * CH)
        conv = sums[0][n] + sums[1][n] + sums[2][n] + sums[3][n] + sums[4][n]
        proj = sums[5][n] + sums[6][n] + sums[7][n]
        line_ref[0:1, lanes] = jnp.sum(conv, axis=0, keepdims=True)
        line_ref[1:2, lanes] = jnp.sum(proj, axis=0, keepdims=True)
    message = line_ref[...]
    for peer in range(32):
        msg_ref[peer] = message


def moments_call(arr, w_own, sc, sp):
    vmem = pl.BlockSpec(memory_space=pltpu.VMEM)
    return pl.pallas_call(
        moments_kernel,
        out_shape=(
            jax.ShapeDtypeStruct((32, 2, 3 * CH), F32),
            jax.ShapeDtypeStruct((8, CH), F32),
        ),
        in_specs=[vmem] * 4,
        out_specs=(vmem,) * 2,
        scratch_shapes=[pltpu.VMEM((2, 3 * CH), F32)],
        compiler_params=small(),
        name="moments",
    )(arr, w_own, sc, sp)


def update_kernel(
    stat_ref, own_ref, other_ref, cw_ref, cm_ref, pw_ref, pm_ref, sc_ref, sp_ref,
    cg_ref, pg_ref, ncw_ref, ncm_ref, npw_ref, npm_ref,
):
    first = lax.axis_index("rows") == 0
    from_low, from_high = stat_ref[0], stat_ref[1]
    for k in range(2, 32, 2):
        from_low = from_low + stat_ref[k]
        from_high = from_high + stat_ref[k + 1]
    from_both = from_low + from_high

    def line(total, row, n):
        return total[row : row + 1, n * CH : (n + 1) * CH]

    own = own_ref[...]
    other = other_ref[...]
    low = jnp.where(first, own, other)
    high = jnp.where(first, other, own)

    def update(weight, mom, grad, sums, stat, gain, fan):
        grad_sum, grad_proj, grad_square = sums
        mean, factor, spread, weight_sq = stat
        one = gain * factor
        two = gain * factor * factor * factor * grad_proj
        raw = one * (grad - grad_sum * (1.0 / fan)) - two * (weight - mean)
        square = (
            one * one * (grad_square - grad_sum * grad_sum * (1.0 / fan))
            - 2.0 * one * two * grad_proj
            + two * two * spread
        )
        square = jnp.maximum(square, 0.0)
        clip = jnp.minimum(1.0, clip_ratio * jnp.sqrt(weight_sq) * lax.rsqrt(square + norm_eps))
        clipped = raw * clip
        new = momentum_rate * mom + clipped
        return weight - learn_rate * (clipped + momentum_rate * new), new

    conv_sums = [line(from_both, 0, n) for n in range(3)]
    conv_stat = [sc_ref[n : n + 1, :] for n in range(4)]
    for rows, grad in ((slice(0, 5), low[0:5, :]), (slice(5, 9), high[0:4, :])):
        weight, mom = update(
            cw_ref[rows, :], cm_ref[rows, :], grad, conv_sums, conv_stat, cg_ref[...], CONV_FAN
        )
        ncw_ref[rows, :] = weight
        ncm_ref[rows, :] = mom
    for part, (block, total) in enumerate(((low, from_low), (high, from_high))):
        lanes = slice(part * CH, (part + 1) * CH)
        weight, mom = update(
            pw_ref[:, lanes], pm_ref[:, lanes], block[5:8, :],
            [line(total, 1, n) for n in range(3)],
            [sp_ref[n : n + 1, lanes] for n in range(4)], pg_ref[:, lanes], PROJ_FAN,
        )
        npw_ref[:, lanes] = weight
        npm_ref[:, lanes] = mom


def update_call(*args):
    vmem = pl.BlockSpec(memory_space=pltpu.VMEM)
    return pl.pallas_call(
        update_kernel,
        out_shape=(
            jax.ShapeDtypeStruct((9, CH), F32),
            jax.ShapeDtypeStruct((9, CH), F32),
            jax.ShapeDtypeStruct((3, OUT), F32),
            jax.ShapeDtypeStruct((3, OUT), F32),
        ),
        in_specs=[vmem] * len(args),
        out_specs=(vmem,) * 4,
        compiler_params=small(),
        name="update",
    )(*args)


def swap(a, axis):
    return lax.ppermute(a, axis, [(0, 1), (1, 0)])


def copies(a, axis):
    n = lax.axis_size(axis)
    return lax.all_to_all(jnp.broadcast_to(a[None], (n, *a.shape)), axis, 0, 0, tiled=True)


def local(
    block_input, output_grad, conv_weight, conv_gain, conv_momentum, proj_weight, proj_gain,
    proj_momentum,
):
    cw, cm, pw, pm = conv_weight.T, conv_momentum.T, proj_weight.T, proj_momentum.T
    cg, pg = conv_gain.reshape(1, CH), proj_gain.reshape(1, OUT)
    x, og = block_input[0], output_grad[0]

    mine, edge = pack_call(cw, pw, x, og)
    halo = swap(edge, "rows")
    w_own = lax.all_to_all(mine, "z", 0, 0, tiled=True)
    w_own, halo = lax.optimization_barrier((w_own, halo))
    w_own = w_own.swapaxes(0, 1).reshape(64, CH)
    wa = copies(w_own, PLANE).reshape(1024, CH)
    wb = swap(wa, "core")
    acat, og9 = patches_call(x, og, halo)
    send, sc, sp, wcb, pp, wc, wp = main_call(wa, wb, acat, og9, cg, pg)
    own = own_call(wc, wp)

    pair = (own + swap(send, "core").astype(F32)).astype(BF16).reshape(16, 64, CH)
    pair, pp = lax.optimization_barrier((pair, pp))
    input_grad = input_call(x, wcb, pp)
    plane = lax.all_to_all(pair, PLANE, 0, 0, tiled=True).astype(F32).sum(axis=0).astype(BF16)
    arr = copies(plane, "z")
    msg, blk = moments_call(arr, w_own, sc, sp)
    other = swap(blk, "rows")
    stat = lax.all_to_all(msg, ("y", "x", "core", "rows"), 0, 0, tiled=True)
    ncw, ncm, npw, npm = update_call(
        stat, blk, other, cw, cm, pw, pm, sc, sp, cg, pg
    )
    return input_grad[None], ncw.T, ncm.T, npw.T, npm.T


def solution(mesh):
    split = Mesh(
        mesh.devices.reshape(8, 4, 2, 2, mesh.shape["rows"]), ("z", "y", "x", "core", "rows")
    )
    maps = P(BATCH, "rows", None, None)
    columns = P(None, BATCH)
    return jax.shard_map(
        local,
        mesh=split,
        in_specs=(maps, maps, columns, P(), columns, columns, P(), columns),
        out_specs=(maps, columns, columns, columns, columns),
        check_vma=False,
    )
```
